32 devices in a mesh: row: 8 (over y, x, core), col: 4 (over z).
Axes of the slice: x: 2, y: 2, z: 4, core: 2. Of those that a mesh axis runs over, the one named last changes fastest.
Arguments:
- samples: bfloat16 [1536, 16384], P('col', 'row'), may hold values from -24 to 24
- omega: float32 [16384, 8, 4, 512], P('row', None, 'col'), may hold values from -0.4 to 2, as said below
- sign_mask: int32 [16384, 8, 4, 512], P('row', None, 'col'), may hold values from -1 to 1, as said below
- step_size: float32 [1], replicated, may hold values from 0.3 to 1
Outputs:
- next_omega: float32 [16384, 8, 4, 512], P('row', None, 'col')
The draws below stay inside these ranges and needn't reach their ends.
Inputs may be any that keep to these rules, and one draw needn't show every extreme that they name: sign_mask is symmetric as a 16384 x 16384 matrix, holds only -1, 0 and 1, and is 1 on the diagonal. omega is symmetric as a 16384 x 16384 matrix, its diagonal lies in 0.5 to 2, and each off-diagonal entry is 0 or has the sign that sign_mask allows.
All inputs are finite; a program needn't handle non-finite values.
Results may differ from the reference program's by a relative error of at most 0.0041.
Values may be sent and summed in bfloat16 or wider, within the bound.
No kernel may reach another device: no remote copies, remote signals or barrier semaphores. Data moves between devices by JAX's collectives and lax.ppermute only.
A program may use at most 384 MiB of HBM per device.

```python
import math
import jax
import jax.numpy as jnp
from jax import lax

VARS = 16384
SAMPLES = 1536
N_ROW = 8
N_COL = 4


def sign_pattern(key):
    levels = jax.random.randint(jax.random.fold_in(key, 11), (VARS, VARS), 0, 3) - 1
    upper = jnp.triu(levels, 1)
    return upper + upper.T + jnp.eye(VARS, dtype=jnp.int32)


def draw_sign_mask(key, part):
    return sign_pattern(key).reshape(VARS, N_ROW, N_COL, VARS // (N_ROW * N_COL)).astype(jnp.int32)


def draw_omega(key, part):
    pattern = sign_pattern(key).astype(jnp.float32)
    mag_key = jax.random.fold_in(key, 12)
    diag_key = jax.random.fold_in(key, 13)
    magnitude = jnp.minimum(0.1 * jnp.abs(jax.random.normal(mag_key, (VARS, VARS), jnp.float32)), 0.4)
    diagonal = jnp.exp(jax.random.uniform(diag_key, (VARS,), jnp.float32, math.log(0.5), math.log(2.0)))
    magnitude = jnp.triu(magnitude, 1)
    magnitude = magnitude + magnitude.T
    full_matrix = pattern * magnitude + jnp.diag(diagonal)
    return full_matrix.reshape(VARS, N_ROW, N_COL, VARS // (N_ROW * N_COL)).astype(jnp.float32)


def draw_samples(key, part):
    col_scale = jnp.exp(jax.random.uniform(jax.random.fold_in(key, 21), (VARS,), jnp.float32, math.log(0.4), math.log(4.0)))
    values = jnp.clip(jax.random.normal(jax.random.fold_in(key, 22), (SAMPLES, VARS), jnp.float32), -6.0, 6.0) * col_scale[None, :]
    return values.astype(jnp.bfloat16)


def setup_inputs(seed: int = 0) -> dict:
    arg_keys = jax.random.split(jax.random.key(seed), 5)
    samples = draw_samples(jax.random.fold_in(arg_keys[4], 71), 0)
    omega = draw_omega(jax.random.fold_in(arg_keys[4], 71), 0)
    sign_mask = draw_sign_mask(jax.random.fold_in(arg_keys[4], 71), 0)
    step_size = jnp.clip(jnp.exp(jax.random.uniform(arg_keys[3], (1,), jnp.float32, math.log(0.3), math.log(1.0))), 0.3, 1.0)
    return {"samples": samples, "omega": omega, "sign_mask": sign_mask, "step_size": step_size}


penalty = 0.05

def update(previous, smooth, row_scale, col_scale, sign_grid, on_diagonal, step_value):
    step_grid = step_value * lax.rsqrt(row_scale * col_scale)
    trial_value = previous - step_grid * smooth
    raised = jnp.maximum(trial_value - penalty * step_grid, 0.0)
    lowered = jnp.minimum(trial_value + penalty * step_grid, 0.0)
    off_value = jnp.where(sign_grid == 1, raised, jnp.where(sign_grid == -1, lowered, 0.0))
    diag_value = 0.5 * (trial_value + jnp.sqrt(trial_value * trial_value + 4.0 * step_grid))
    return jnp.where(on_diagonal, diag_value, off_value)

def reference(samples, omega, sign_mask, step_size):
    precision = omega.reshape(VARS, VARS)
    sign_grid = sign_mask.reshape(VARS, VARS)
    squares = lax.optimization_barrier(jnp.sum(jnp.square(samples.astype(jnp.float32)), axis=0)) / SAMPLES + 1e-06
    scales = lax.optimization_barrier(squares.astype(jnp.bfloat16)).astype(jnp.float32)
    product = jnp.dot(samples, precision.astype(jnp.bfloat16), preferred_element_type=jnp.float32).astype(jnp.bfloat16)
    cross_term = lax.dot_general(samples, product, (((0,), (0,)), ((), ())), preferred_element_type=jnp.float32) / SAMPLES
    block_size = VARS // N_ROW

    def one_block(block_index):
        first_row = block_index * block_size
        row_part = lax.dynamic_slice_in_dim(cross_term, first_row, block_size, 0)
        col_part = lax.dynamic_slice_in_dim(cross_term, first_row, block_size, 1)
        smooth = 0.5 * (row_part + col_part.T)
        row_scale = lax.dynamic_slice_in_dim(scales, first_row, block_size, 0)
        old_rows = lax.dynamic_slice_in_dim(precision, first_row, block_size, 0)
        sign_rows = lax.dynamic_slice_in_dim(sign_grid, first_row, block_size, 0)
        row_ids = first_row + lax.broadcasted_iota(jnp.int32, (block_size, VARS), 0)
        col_ids = lax.broadcasted_iota(jnp.int32, (block_size, VARS), 1)
        return update(old_rows, smooth, row_scale[:, None], scales[None, :], sign_rows, row_ids == col_ids, step_size[0])
    updated = lax.map(one_block, jnp.arange(N_ROW, dtype=jnp.int32))
    return updated.reshape(VARS, N_ROW, N_COL, VARS // (N_ROW * N_COL))
```

```python
import functools

import jax
import jax.numpy as jnp
from jax import lax
from jax.experimental import pallas as pl
from jax.experimental.pallas import tpu as pltpu
from jax.sharding import PartitionSpec as P

PENALTY = 0.05
LANES = 128
SUBS = 8
CHUNKS = 2
MIB = 1 << 20


def convert_kernel(omega_ref, out_ref):
    rows = omega_ref.shape[0]
    blocks, _, width = out_ref.shape
    flat = omega_ref.reshape(rows * SUBS, LANES)
    per_block = width // LANES
    for c in range(SUBS):
        piece = flat[pl.ds(c, rows, stride=SUBS), :].astype(jnp.bfloat16)
        lane = (c % per_block) * LANES
        out_ref[c // per_block, :, lane : lane + LANES] = piece


def convert(omega3, group_count, sub_width):
    row_total, lane_tiles, _ = omega3.shape
    tile = min(512, row_total)
    blocks = SUBS * LANES // sub_width
    return pl.pallas_call(
        convert_kernel,
        grid=(row_total // tile, lane_tiles // SUBS),
        in_specs=[pl.BlockSpec((tile, SUBS, LANES), lambda i, j: (i, j, 0))],
        out_specs=pl.BlockSpec((blocks, tile, sub_width), lambda i, j: (j, i, 0)),
        out_shape=jax.ShapeDtypeStruct((group_count, row_total, sub_width), jnp.bfloat16),
        compiler_params=pltpu.CompilerParams(vmem_limit_bytes=32 * MIB),
        cost_estimate=pl.CostEstimate(flops=0, bytes_accessed=omega3.size * 6, transcendentals=0),
        name="omega_to_bf16",
    )(omega3)


def partial_kernel(x_ref, w_ref, out_ref):
    out_ref[0] = jnp.dot(x_ref[...], w_ref[0], preferred_element_type=jnp.float32)


def partial_product(x_rows, weights):
    count, depth = x_rows.shape
    group_count, _, sub_width = weights.shape
    return pl.pallas_call(
        partial_kernel,
        grid=(group_count,),
        in_specs=[
            pl.BlockSpec((count, depth), lambda g: (0, 0)),
            pl.BlockSpec((1, depth, sub_width), lambda g: (g, 0, 0)),
        ],
        out_specs=pl.BlockSpec((1, count, sub_width), lambda g: (g, 0, 0)),
        out_shape=jax.ShapeDtypeStruct((group_count, count, sub_width), jnp.float32),
        compiler_params=pltpu.CompilerParams(vmem_limit_bytes=40 * MIB),
        cost_estimate=pl.CostEstimate(
            flops=2 * count * depth * group_count * sub_width,
            bytes_accessed=2 * (x_rows.size + weights.size + count * group_count * sub_width),
            transcendentals=0,
        ),
        name="partial_product",
    )(x_rows, weights)


def turn_kernel(in_ref, out_ref):
    out_ref[...] = in_ref[...].T


def turn(rows, width):
    count, total = rows.shape
    return pl.pallas_call(
        turn_kernel,
        grid=(total // width,),
        in_specs=[pl.BlockSpec((count, width), lambda i: (0, i))],
        out_specs=pl.BlockSpec((width, count), lambda i: (i, 0)),
        out_shape=jax.ShapeDtypeStruct((total, count), rows.dtype),
        compiler_params=pltpu.CompilerParams(vmem_limit_bytes=16 * MIB),
        cost_estimate=pl.CostEstimate(
            flops=0, bytes_accessed=4 * rows.size, transcendentals=0
        ),
        name="turn",
    )(rows)


def final_kernel(pairs, sub_width, scale, place_ref, *refs):
    lhs = refs[:pairs]
    rhs = refs[pairs : 2 * pairs]
    omega_ref, sign_ref, row_ref, col_ref, out_ref, smooth_ref = refs[2 * pairs :]
    rows = omega_ref.shape[0]
    omega = omega_ref.reshape(rows * SUBS, LANES)
    signs = sign_ref.reshape(rows * SUBS, LANES)
    out = out_ref.reshape(rows * SUBS, LANES)
    per_block = sub_width // LANES
    blocks = SUBS // per_block
    step = min(sub_width, 256)
    row_rate = jnp.broadcast_to(row_ref[...], (rows, LANES))
    for b in range(blocks):
        for first in range(0, sub_width, step):
            total = None
            for left, right in zip(lhs, rhs):
                term = jnp.dot(
                    left[...], right[b, :, first : first + step], preferred_element_type=jnp.float32
                )
                total = term if total is None else total + term
            at = b * sub_width + first
            smooth_ref[:, at : at + step] = total * scale
            for lane in range(0, step, LANES):
                c = (at + lane) // LANES
                spot = pl.ds(c, rows, stride=SUBS)
                rate = row_rate * col_ref[b, :, first + lane : first + lane + LANES]
                trial = omega[spot, :] - rate * (total[:, lane : lane + LANES] * scale)
                sign = signs[spot, :]
                shift = PENALTY * rate
                raised = jnp.maximum(trial - shift, 0.0)
                lowered = jnp.minimum(trial + shift, 0.0)
                out[spot, :] = jnp.where(sign == 1, raised, jnp.where(sign == -1, lowered, 0.0))

    first_row = pl.program_id(1) * rows
    for b in range(blocks):
        row_start = place_ref[1] * sub_width - first_row
        here = jnp.logical_and(
            pl.program_id(0) * blocks + b == place_ref[0],
            jnp.logical_and(row_start >= 0, row_start < rows),
        )

        @pl.when(here)
        def _():
            for lane in range(0, sub_width, LANES):
                c = (b * sub_width + lane) // LANES
                spot = pl.ds(c, rows, stride=SUBS)
                rate = row_rate * col_ref[b, :, lane : lane + LANES]
                trial = omega[spot, :] - rate * smooth_ref[:, c * LANES : (c + 1) * LANES]
                value = 0.5 * (trial + jnp.sqrt(trial * trial + 4.0 * rate))
                row_ids = lax.broadcasted_iota(jnp.int32, (rows, LANES), 0)
                col_ids = lax.broadcasted_iota(jnp.int32, (rows, LANES), 1) + (lane + row_start)
                out[spot, :] = jnp.where(row_ids == col_ids, value, out[spot, :])


def final_update(lhs, rhs, omega3, sign3, row_rate, col_rate, place, sub_width, scale):
    row_total, lane_tiles, _ = omega3.shape
    tile = min(512, row_total)
    blocks = SUBS * LANES // sub_width
    pairs = len(lhs)
    depth = sum(a.shape[1] for a in lhs)
    grid_block = pl.BlockSpec((tile, SUBS, LANES), lambda j, i, p: (i, j, 0))
    return pl.pallas_call(
        functools.partial(final_kernel, pairs, sub_width, scale),
        grid_spec=pltpu.PrefetchScalarGridSpec(
            num_scalar_prefetch=1,
            grid=(lane_tiles // SUBS, row_total // tile),
            in_specs=[pl.BlockSpec((tile, a.shape[1]), lambda j, i, p: (i, 0)) for a in lhs]
            + [
                pl.BlockSpec((blocks, b.shape[1], sub_width), lambda j, i, p: (j, 0, 0))
                for b in rhs
            ]
            + [
                grid_block,
                grid_block,
                pl.BlockSpec((tile, 1), lambda j, i, p: (i, 0)),
                pl.BlockSpec((blocks, 1, sub_width), lambda j, i, p: (j, 0, 0)),
            ],
            out_specs=grid_block,
            scratch_shapes=[pltpu.VMEM((tile, SUBS * LANES), jnp.float32)],
        ),
        out_shape=jax.ShapeDtypeStruct(omega3.shape, jnp.float32),
        compiler_params=pltpu.CompilerParams(vmem_limit_bytes=56 * MIB),
        cost_estimate=pl.CostEstimate(
            flops=2 * depth * omega3.size, bytes_accessed=omega3.size * 12, transcendentals=0
        ),
        name="final_update",
    )(place, *lhs, *rhs, omega3, sign3, row_rate, col_rate)


def body(samples, omega, sign_mask, step_size):
    row_total, group_count, _, sub_width = omega.shape
    lane_tiles = group_count * sub_width // LANES
    row_index = lax.axis_index("row")
    col_index = lax.axis_index("col")
    sample_total = samples.shape[0] * lax.axis_size("col")
    omega3 = omega.reshape(row_total, lane_tiles, LANES)
    sign3 = sign_mask.reshape(row_total, lane_tiles, LANES)

    weights = convert(omega3, group_count, sub_width)
    part = samples.shape[0] // CHUNKS
    x_rows = [
        lax.all_gather(samples[k * part : (k + 1) * part], "col", axis=0, tiled=True)
        for k in range(CHUNKS)
    ]
    x_cols, y_rows, y_cols = [], [], []
    for x in x_rows:
        partial = partial_product(x, weights)
        share = lax.psum_scatter(partial, "row", scatter_dimension=0, tiled=False)
        share = lax.optimization_barrier(share).astype(jnp.bfloat16)
        y_rows.append(lax.all_gather(turn(share, sub_width), "col", axis=0, tiled=True))
        y_cols.append(lax.all_gather(share, "row", axis=0, tiled=False))
        own = lax.dynamic_slice_in_dim(x, col_index * sub_width, sub_width, 1)
        x_cols.append(lax.all_gather(own, "row", axis=0, tiled=False))

    def mean_square(pieces, axis):
        total = sum(jnp.sum(jnp.square(p.astype(jnp.float32)), axis=axis) for p in pieces)
        total = lax.optimization_barrier(total) / sample_total + 1e-06
        return lax.optimization_barrier(total.astype(jnp.bfloat16)).astype(jnp.float32)

    row_rate = (step_size[0] * lax.rsqrt(mean_square(x_rows, 0)))[:, None]
    col_rate = lax.rsqrt(mean_square(x_cols, 1))[:, None, :]
    place = jnp.stack([row_index, col_index]).astype(jnp.int32)
    updated = final_update(
        [turn(x, sub_width) for x in x_rows] + y_rows,
        y_cols + x_cols,
        omega3,
        sign3,
        row_rate,
        col_rate,
        place,
        sub_width,
        0.5 / sample_total,
    )
    return updated.reshape(omega.shape)


def solution(mesh):
    in_specs = (P("col", "row"), P("row", None, "col", None), P("row", None, "col", None), P())
    out_specs = P("row", None, "col", None)
    return jax.shard_map(body, mesh=mesh, in_specs=in_specs, out_specs=out_specs, check_vma=False)
```

```python
import functools

import jax
import jax.numpy as jnp
from jax import lax
from jax.experimental import pallas as pl
from jax.experimental.pallas import tpu as pltpu
from jax.sharding import PartitionSpec as P

PENALTY = 0.05
LANES = 128
SUBS = 8
GROUPS = 2
MIB = 1 << 20


def convert_kernel(omega_ref, out_ref):
    rows = omega_ref.shape[0]
    blocks, _, width = out_ref.shape
    flat = omega_ref.reshape(rows * SUBS, LANES)
    per_block = width // LANES
    for c in range(SUBS):
        piece = flat[pl.ds(c, rows, stride=SUBS), :].astype(jnp.bfloat16)
        lane = (c % per_block) * LANES
        out_ref[c // per_block, :, lane : lane + LANES] = piece


def convert(omega3, group_count, sub_width):
    row_total, lane_tiles, _ = omega3.shape
    tile = min(512, row_total)
    blocks = SUBS * LANES // sub_width
    return pl.pallas_call(
        convert_kernel,
        grid=(row_total // tile, lane_tiles // SUBS),
        in_specs=[pl.BlockSpec((tile, SUBS, LANES), lambda i, j: (i, j, 0))],
        out_specs=pl.BlockSpec((blocks, tile, sub_width), lambda i, j: (j, i, 0)),
        out_shape=jax.ShapeDtypeStruct((group_count, row_total, sub_width), jnp.bfloat16),
        compiler_params=pltpu.CompilerParams(vmem_limit_bytes=32 * MIB),
        cost_estimate=pl.CostEstimate(flops=0, bytes_accessed=omega3.size * 6, transcendentals=0),
        name="omega_to_bf16",
    )(omega3)


def turn_kernel(in_ref, out_ref):
    out_ref[...] = in_ref[...].T


def turn(rows, width):
    count, total = rows.shape
    return pl.pallas_call(
        turn_kernel,
        grid=(total // width,),
        in_specs=[pl.BlockSpec((count, width), lambda i: (0, i))],
        out_specs=pl.BlockSpec((width, count), lambda i: (i, 0)),
        out_shape=jax.ShapeDtypeStruct((total, count), rows.dtype),
        compiler_params=pltpu.CompilerParams(vmem_limit_bytes=16 * MIB),
        cost_estimate=pl.CostEstimate(
            flops=0, bytes_accessed=4 * rows.size, transcendentals=0
        ),
        name="turn",
    )(rows)


def tie(values, done):
    return lax.optimization_barrier((values, done))[0] if done else values


def multiply_rows(x_refs, weight):
    return [jnp.dot(x[...], weight, preferred_element_type=jnp.float32) for x in x_refs]


def sent_kernel(count, order_ref, *refs):
    x_refs, w_ref, out_ref = refs[:count], refs[count], refs[count + 1]
    rows = x_refs[0].shape[0]
    for k, piece in enumerate(multiply_rows(x_refs, w_ref[0])):
        out_ref[0, k * rows : (k + 1) * rows, :] = piece.astype(jnp.bfloat16)


def reversed_bits(value, bits):
    return sum(((value >> b) & 1) << (bits - 1 - b) for b in range(bits))


def kept_kernel(count, bits, order_ref, *refs):
    x_refs, w_ref, other_ref = refs[:count], refs[count], refs[count + 1]
    halves = (refs[count + 2 : count + 4], refs[count + 4 : count + 6])
    rows = x_refs[0].shape[0]
    step = pl.program_id(0)
    split = 1 << (bits - 1)
    sums = []
    for k, piece in enumerate(multiply_rows(x_refs, w_ref[0])):
        sums.append(piece + other_ref[0, k * rows : (k + 1) * rows, :].astype(jnp.float32))
    for relative in range(1 << bits):

        @pl.when(step == relative)
        def _():
            for h, (sent_ref, kept_ref) in enumerate(halves):
                place = relative if h else reversed_bits(relative, bits)
                target = sent_ref if place >= split else kept_ref
                for k in range(count // 2):
                    piece = sums[h * (count // 2) + k].astype(target.dtype)
                    target[place % split, k * rows : (k + 1) * rows, :] = piece


def pair_products(xs, weights, order_sent, order_kept, row_partner, beside):
    count = len(xs)
    rows, depth = xs[0].shape
    group_count, _, width = weights.shape
    blocks = group_count // 2
    bits = blocks.bit_length() - 1
    total_rows = count * rows
    x_spec = pl.BlockSpec((rows, depth), lambda g, order: (0, 0))
    w_spec = pl.BlockSpec((1, depth, width), lambda g, order: (order[g], 0, 0))
    block_spec = pl.BlockSpec((1, total_rows, width), lambda g, order: (g, 0, 0))
    cost = pl.CostEstimate(
        flops=2 * total_rows * depth * blocks * width,
        bytes_accessed=weights.size + 2 * count * xs[0].size + 2 * blocks * total_rows * width,
        transcendentals=0,
    )
    params = pltpu.CompilerParams(vmem_limit_bytes=48 * MIB)
    sent = pl.pallas_call(
        functools.partial(sent_kernel, count),
        grid_spec=pltpu.PrefetchScalarGridSpec(
            num_scalar_prefetch=1,
            grid=(blocks,),
            in_specs=[x_spec] * count + [w_spec],
            out_specs=block_spec,
        ),
        out_shape=jax.ShapeDtypeStruct((blocks, total_rows, width), jnp.bfloat16),
        compiler_params=params,
        cost_estimate=cost,
        name="products_sent",
    )(order_sent, *xs, weights)
    other = tie(lax.ppermute(sent, "row", row_partner(1)), beside(0))
    half = (blocks // 2, total_rows // 2, width)
    half_spec = pl.BlockSpec(half, lambda g, order: (0, 0, 0))
    outs = pl.pallas_call(
        functools.partial(kept_kernel, count, bits),
        grid_spec=pltpu.PrefetchScalarGridSpec(
            num_scalar_prefetch=1,
            grid=(blocks,),
            in_specs=[x_spec] * count + [w_spec, block_spec],
            out_specs=[half_spec] * 4,
        ),
        out_shape=[
            jax.ShapeDtypeStruct(half, jnp.bfloat16),
            jax.ShapeDtypeStruct(half, jnp.float32),
        ]
        * 2,
        compiler_params=params,
        cost_estimate=cost,
        name="products_kept",
    )(order_kept, *xs, weights, other)
    return [(outs[0], outs[1]), (outs[2], outs[3])]


def halve_kernel(split, *refs):
    for h in range(2):
        kept_ref, other_ref, next_sent, next_kept = refs[2 * h], refs[2 * h + 1], refs[4 + 2 * h], refs[5 + 2 * h]
        next_kept[...] = kept_ref[:split] + other_ref[:split].astype(jnp.float32)
        total = kept_ref[split:] + other_ref[split:].astype(jnp.float32)
        next_sent[...] = total.astype(jnp.bfloat16)


def halve(pieces, others):
    kept = pieces[0][1]
    split = kept.shape[0] // 2
    shape = (split,) + kept.shape[1:]
    outs = pl.pallas_call(
        functools.partial(halve_kernel, split),
        out_shape=[
            jax.ShapeDtypeStruct(shape, jnp.bfloat16),
            jax.ShapeDtypeStruct(shape, jnp.float32),
        ]
        * 2,
        compiler_params=pltpu.CompilerParams(vmem_limit_bytes=32 * MIB),
        cost_estimate=pl.CostEstimate(flops=0, bytes_accessed=18 * kept.size, transcendentals=0),
        name="halve",
    )(pieces[0][1], others[0], pieces[1][1], others[1])
    return [(outs[0], outs[1]), (outs[2], outs[3])]


def share_kernel(*refs):
    share_ref, turned_ref = refs[4:]
    rows = refs[0].shape[1]
    for h in range(2):
        total = refs[2 * h][0] + refs[2 * h + 1][0].astype(jnp.float32)
        share_ref[h * rows : (h + 1) * rows, :] = total.astype(jnp.bfloat16)
    turned_ref[...] = share_ref[...].T


def finish_share(pieces, others):
    _, rows, width = pieces[0][1].shape
    return pl.pallas_call(
        share_kernel,
        out_shape=[
            jax.ShapeDtypeStruct((2 * rows, width), jnp.bfloat16),
            jax.ShapeDtypeStruct((width, 2 * rows), jnp.bfloat16),
        ],
        compiler_params=pltpu.CompilerParams(vmem_limit_bytes=24 * MIB),
        cost_estimate=pl.CostEstimate(
            flops=0, bytes_accessed=20 * rows * width, transcendentals=0
        ),
        name="share",
    )(pieces[0][1], others[0], pieces[1][1], others[1])


def sum_over_rows(xs, weights, order_sent, order_kept, row_partner, beside):
    pieces = pair_products(xs, weights, order_sent, order_kept, row_partner, beside)
    bits = weights.shape[0].bit_length() - 2
    for level in range(bits):
        masks = (2 << level, 1 << (bits - level))
        others = [
            lax.ppermute(sent, "row", row_partner(mask)) for (sent, _), mask in zip(pieces, masks)
        ]
        others = tie(others, beside(level + 1))
        if level < bits - 1:
            pieces = halve(pieces, others)
    share, turned = finish_share(pieces, others)
    return share, turned


def final_kernel(count, places, sub_width, scale, diagonal, with_previous, info_ref, *refs):
    groups = 2 * GROUPS
    lhs = refs[:count]
    rhs = refs[count : count + groups]
    omega_ref, sign_ref, row_ref, col_ref = refs[count + groups : count + groups + 4]
    out_ref, lhs_ref, smooth_ref = refs[count + groups + 4 + with_previous :]
    rows = omega_ref.shape[0]

    @pl.when(pl.program_id(0) == 0)
    def _():
        for k, source, target, size in places:
            lhs_ref[:, target : target + size] = lhs[k][:, source : source + size]

    omega = omega_ref.reshape(rows * SUBS, LANES)
    signs = sign_ref.reshape(rows * SUBS, LANES)
    out = out_ref.reshape(rows * SUBS, LANES)
    per_block = sub_width // LANES
    blocks = SUBS // per_block
    step = min(sub_width, 256)
    row_rate = jnp.broadcast_to(row_ref[...], (rows, LANES))
    row_smooth = row_rate * scale
    row_shift = row_rate * PENALTY
    for b in range(blocks):
        for first in range(0, sub_width, step):
            right = jnp.concatenate([r[b, :, first : first + step] for r in rhs], axis=0)
            total = jnp.dot(lhs_ref[...], right, preferred_element_type=jnp.float32)
            at = b * sub_width + first
            if diagonal:
                smooth_ref[:, at : at + step] = total
            for lane in range(0, step, LANES):
                spot = pl.ds((at + lane) // LANES, rows, stride=SUBS)
                col_rate = col_ref[b, :, first + lane : first + lane + LANES]
                trial = omega[spot, :] - (row_smooth * col_rate) * total[:, lane : lane + LANES]
                sign = signs[spot, :].astype(jnp.float32)
                out[spot, :] = sign * jnp.maximum(sign * trial - row_shift * col_rate, 0.0)

    if diagonal:
        for b in range(blocks):

            @pl.when(pl.program_id(0) * blocks + b == info_ref[1])
            def _():
                for lane in range(0, sub_width, LANES):
                    c = (b * sub_width + lane) // LANES
                    spot = pl.ds(c, rows, stride=SUBS)
                    rate = row_rate * col_ref[b, :, lane : lane + LANES]
                    smooth = smooth_ref[:, c * LANES : (c + 1) * LANES] * scale
                    trial = omega[spot, :] - rate * smooth
                    value = 0.5 * (trial + jnp.sqrt(trial * trial + 4.0 * rate))
                    row_ids = lax.broadcasted_iota(jnp.int32, (rows, LANES), 0)
                    col_ids = lax.broadcasted_iota(jnp.int32, (rows, LANES), 1) + lane
                    out[spot, :] = jnp.where(row_ids == col_ids, value, out[spot, :])


def final_update(lhs, places, rhs, omega3, sign3, row_rate, col_rate, info, previous, scale):
    row_total, lane_tiles, _ = omega3.shape
    _, sample_count, sub_width = rhs[0].shape
    tile = sub_width
    blocks = SUBS * LANES // sub_width
    depth = sample_count * len(rhs)
    diagonal = previous is None
    grid_block = pl.BlockSpec((tile, SUBS, LANES), lambda j, p: (p[0], j, 0))
    lhs_specs = [
        pl.BlockSpec((tile, a.shape[1]), (lambda j, p: (p[0], 0)) if by_row else (lambda j, p: (0, 0)))
        for a, by_row in lhs
    ]
    operands = [a for a, _ in lhs] + list(rhs) + [omega3, sign3, row_rate, col_rate]
    specs = (
        lhs_specs
        + [pl.BlockSpec((blocks, sample_count, sub_width), lambda j, p: (j, 0, 0)) for _ in rhs]
        + [
            grid_block,
            grid_block,
            pl.BlockSpec((tile, 1), lambda j, p: (p[0], 0)),
            pl.BlockSpec((blocks, 1, sub_width), lambda j, p: (j, 0, 0)),
        ]
    )
    aliases = {}
    if previous is not None:
        operands.append(previous)
        specs.append(pl.BlockSpec(memory_space=pl.ANY))
        aliases = {len(operands): 0}
    elements = tile * lane_tiles * LANES
    return pl.pallas_call(
        functools.partial(
            final_kernel, len(lhs), places, sub_width, scale, diagonal, previous is not None
        ),
        grid_spec=pltpu.PrefetchScalarGridSpec(
            num_scalar_prefetch=1,
            grid=(lane_tiles // SUBS,),
            in_specs=specs,
            out_specs=grid_block,
            scratch_shapes=[
                pltpu.VMEM((tile, depth), jnp.bfloat16),
                pltpu.VMEM((tile, SUBS * LANES if diagonal else LANES), jnp.float32),
            ],
        ),
        out_shape=jax.ShapeDtypeStruct(omega3.shape, jnp.float32),
        input_output_aliases=aliases,
        compiler_params=pltpu.CompilerParams(vmem_limit_bytes=56 * MIB),
        cost_estimate=pl.CostEstimate(
            flops=2 * depth * elements, bytes_accessed=elements * 16, transcendentals=0
        ),
        name="final_update",
    )(info, *operands)


def body(samples, omega, sign_mask, step_size):
    row_total, group_count, _, sub_width = omega.shape
    lane_tiles = group_count * sub_width // LANES
    row_count = lax.axis_size("row")
    col_count = lax.axis_size("col")
    row_index = lax.axis_index("row").astype(jnp.int32)
    col_index = lax.axis_index("col").astype(jnp.int32)
    part = samples.shape[0]
    sample_total = part * col_count
    per_group = col_count // GROUPS
    omega3 = omega.reshape(row_total, lane_tiles, LANES)
    sign3 = sign_mask.reshape(row_total, lane_tiles, LANES)

    def row_partner(mask):
        return [(r, r ^ mask) for r in range(row_count)]

    ring = [(c, (c + 1) % col_count) for c in range(col_count)]
    relative = jnp.arange(row_count // 2, dtype=jnp.int32)
    order_kept = ((row_index >> 1) ^ relative) * 2 + (row_index & 1)
    order_sent = order_kept ^ 1

    xs, x_turned = [samples], []
    weights = convert(omega3, group_count, sub_width)
    x_cols, y_cols, y_rings = [], [], []

    def advance(ring_pieces):
        ring_pieces.append(lax.ppermute(ring_pieces[-1], "col", ring))
        return ring_pieces[-1]

    for k in range(GROUPS):
        first = k * per_group
        while len(xs) < first + per_group:
            advance(xs)
            if not first:
                xs[-1] = tie(xs[-1], [weights])
        group = xs[first : first + per_group]
        own = [lax.dynamic_slice_in_dim(x, col_index * sub_width, sub_width, 1) for x in group]
        x_cols.append(lax.all_gather(jnp.concatenate(own, axis=0), "row", axis=0, tiled=False))

        def beside(exchange):
            done = []
            if exchange == 0:
                x_turned.extend(turn(x, sub_width) for x in group)
                done.extend(x_turned[first:])
                done.extend(x_cols[:-1])
            if exchange == 1:
                done.extend(y_cols)
                if len(xs) < col_count:
                    done.append(advance(xs))
            if y_rings and len(y_rings[0]) < col_count:
                done.append(advance(y_rings[0]))
            return done

        share, turned = sum_over_rows(
            group, weights, order_sent, order_kept, row_partner, beside
        )
        y_cols.append(lax.all_gather(share, "row", axis=0, tiled=False))
        y_rings.append([turned])
    for pieces in y_rings:
        while len(pieces) < col_count:
            advance(pieces)
    y_cols[-1] = tie(y_cols[-1], [pieces[-2] for pieces in y_rings])

    def mean_square(pieces, axis):
        total = sum(jnp.sum(jnp.square(p.astype(jnp.float32)), axis=axis) for p in pieces)
        total = lax.optimization_barrier(total) / sample_total + 1e-06
        return lax.optimization_barrier(total.astype(jnp.bfloat16)).astype(jnp.float32)

    row_rate = (step_size[0] * lax.rsqrt(mean_square(xs, 0)))[:, None]
    col_rate = lax.rsqrt(mean_square(x_cols, 1))[:, None, :]
    x_places = tuple((s, 0, s * part, part) for s in range(col_count))

    updated = None
    for distance in range(col_count):
        y_places = tuple(
            (
                col_count + s // per_group,
                s % per_group * part,
                sample_total + (s + distance) % col_count * part,
                part,
            )
            for s in range(col_count)
        )
        lhs = [(x, True) for x in x_turned] + [(y[distance], False) for y in y_rings]
        info = jnp.stack([(col_index - distance + col_count) % col_count, row_index])
        updated = final_update(
            lhs,
            x_places + y_places,
            y_cols + x_cols,
            omega3,
            sign3,
            row_rate,
            col_rate,
            info,
            updated,
            0.5 / sample_total,
        )
    return updated.reshape(omega.shape)


def solution(mesh):
    in_specs = (P("col", "row"), P("row", None, "col", None), P("row", None, "col", None), P())
    out_specs = P("row", None, "col", None)
    return jax.shard_map(body, mesh=mesh, in_specs=in_specs, out_specs=out_specs, check_vma=False)
```

```python
import functools

import jax
import jax.numpy as jnp
from jax import lax
from jax.experimental import pallas as pl
from jax.experimental.pallas import tpu as pltpu
from jax.sharding import PartitionSpec as P

PENALTY = 0.05
LANES = 128
SUBS = 8
GROUPS = 2
PIECES = 2
X_STEPS = (1, 2, 1)
MIB = 1 << 20


def convert_kernel(omega_ref, out_ref):
    rows = omega_ref.shape[0]
    blocks, _, width = out_ref.shape
    flat = omega_ref.reshape(rows * SUBS, LANES)
    per_block = width // LANES
    for c in range(SUBS):
        piece = flat[pl.ds(c, rows, stride=SUBS), :].astype(jnp.bfloat16)
        lane = (c % per_block) * LANES
        out_ref[c // per_block, :, lane : lane + LANES] = piece


def convert(omega3, group_count, sub_width):
    row_total, lane_tiles, _ = omega3.shape
    tile = min(512, row_total)
    blocks = SUBS * LANES // sub_width
    return pl.pallas_call(
        convert_kernel,
        grid=(row_total // tile, lane_tiles // SUBS),
        in_specs=[pl.BlockSpec((tile, SUBS, LANES), lambda i, j: (i, j, 0))],
        out_specs=pl.BlockSpec((blocks, tile, sub_width), lambda i, j: (j, i, 0)),
        out_shape=jax.ShapeDtypeStruct((group_count, row_total, sub_width), jnp.bfloat16),
        compiler_params=pltpu.CompilerParams(vmem_limit_bytes=32 * MIB),
        cost_estimate=pl.CostEstimate(flops=0, bytes_accessed=omega3.size * 6, transcendentals=0),
        name="omega_to_bf16",
    )(omega3)


def turn_kernel(*refs):
    refs[-1][...] = jnp.concatenate([r[...] for r in refs[:-1]], axis=0).T


def turn(pieces, width):
    rows, total = pieces[0].shape
    count = rows * len(pieces)
    return pl.pallas_call(
        turn_kernel,
        grid=(total // width,),
        in_specs=[pl.BlockSpec((rows, width), lambda i: (0, i)) for _ in pieces],
        out_specs=pl.BlockSpec((width, count), lambda i: (i, 0)),
        out_shape=jax.ShapeDtypeStruct((total, count), pieces[0].dtype),
        compiler_params=pltpu.CompilerParams(vmem_limit_bytes=16 * MIB),
        cost_estimate=pl.CostEstimate(
            flops=0, bytes_accessed=4 * count * total, transcendentals=0
        ),
        name="turn",
    )(*pieces)


def tie(values, done):
    return lax.optimization_barrier((values, done))[0] if done else values


def multiply_rows(x_refs, weight):
    rows = jnp.concatenate([x[...] for x in x_refs], axis=0)
    return jnp.dot(rows, weight, preferred_element_type=jnp.float32)


def sent_kernel(count, order_ref, *refs):
    x_refs, w_ref, out_ref = refs[:count], refs[count], refs[count + 1]
    out_ref[0] = multiply_rows(x_refs, w_ref[0]).astype(jnp.bfloat16)


def reversed_bits(value, bits):
    return sum(((value >> b) & 1) << (bits - 1 - b) for b in range(bits))


def kept_kernel(count, bits, order_ref, *refs):
    x_refs, w_ref, other_ref = refs[:count], refs[count], refs[count + 1]
    halves = (refs[count + 2 : count + 4], refs[count + 4 : count + 6])
    total = multiply_rows(x_refs, w_ref[0]) + other_ref[0].astype(jnp.float32)
    rows = total.shape[0] // 2
    step = pl.program_id(0)
    split = 1 << (bits - 1)
    for relative in range(1 << bits):

        @pl.when(step == relative)
        def _():
            for h, (sent_ref, kept_ref) in enumerate(halves):
                place = relative if h else reversed_bits(relative, bits)
                target = sent_ref if place >= split else kept_ref
                target[place % split] = total[h * rows : (h + 1) * rows].astype(target.dtype)


def pair_products(xs, weights, order_sent, order_kept, row_partner, beside):
    count = len(xs)
    rows, depth = xs[0].shape
    group_count, _, width = weights.shape
    blocks = group_count // 2
    bits = blocks.bit_length() - 1
    total_rows = count * rows
    x_spec = pl.BlockSpec((rows, depth), lambda g, order: (0, 0))
    w_spec = pl.BlockSpec((1, depth, width), lambda g, order: (order[g], 0, 0))
    block_spec = pl.BlockSpec((1, total_rows, width), lambda g, order: (g, 0, 0))
    cost = pl.CostEstimate(
        flops=2 * total_rows * depth * blocks * width,
        bytes_accessed=weights.size + 2 * count * xs[0].size + 2 * blocks * total_rows * width,
        transcendentals=0,
    )
    params = pltpu.CompilerParams(vmem_limit_bytes=48 * MIB)
    sent = pl.pallas_call(
        functools.partial(sent_kernel, count),
        grid_spec=pltpu.PrefetchScalarGridSpec(
            num_scalar_prefetch=1,
            grid=(blocks,),
            in_specs=[x_spec] * count + [w_spec],
            out_specs=block_spec,
        ),
        out_shape=jax.ShapeDtypeStruct((blocks, total_rows, width), jnp.bfloat16),
        compiler_params=params,
        cost_estimate=cost,
        name="products_sent",
    )(order_sent, *xs, weights)
    other = tie(lax.ppermute(sent, "row", row_partner(1)), beside(0))
    half = (blocks // 2, total_rows // 2, width)
    half_spec = pl.BlockSpec(half, lambda g, order: (0, 0, 0))
    outs = pl.pallas_call(
        functools.partial(kept_kernel, count, bits),
        grid_spec=pltpu.PrefetchScalarGridSpec(
            num_scalar_prefetch=1,
            grid=(blocks,),
            in_specs=[x_spec] * count + [w_spec, block_spec],
            out_specs=[half_spec] * 4,
        ),
        out_shape=[
            jax.ShapeDtypeStruct(half, jnp.bfloat16),
            jax.ShapeDtypeStruct(half, jnp.float32),
        ]
        * 2,
        compiler_params=params,
        cost_estimate=cost,
        name="products_kept",
    )(order_kept, *xs, weights, other)
    return [(outs[0], outs[1]), (outs[2], outs[3])]


def halve_kernel(split, *refs):
    for h in range(2):
        kept_ref, other_ref, next_sent, next_kept = refs[2 * h], refs[2 * h + 1], refs[4 + 2 * h], refs[5 + 2 * h]
        next_kept[...] = kept_ref[:split] + other_ref[:split].astype(jnp.float32)
        total = kept_ref[split:] + other_ref[split:].astype(jnp.float32)
        next_sent[...] = total.astype(jnp.bfloat16)


def halve(pieces, others):
    kept = pieces[0][1]
    split = kept.shape[0] // 2
    shape = (split,) + kept.shape[1:]
    outs = pl.pallas_call(
        functools.partial(halve_kernel, split),
        out_shape=[
            jax.ShapeDtypeStruct(shape, jnp.bfloat16),
            jax.ShapeDtypeStruct(shape, jnp.float32),
        ]
        * 2,
        compiler_params=pltpu.CompilerParams(vmem_limit_bytes=32 * MIB),
        cost_estimate=pl.CostEstimate(flops=0, bytes_accessed=18 * kept.size, transcendentals=0),
        name="halve",
    )(pieces[0][1], others[0], pieces[1][1], others[1])
    return [(outs[0], outs[1]), (outs[2], outs[3])]


def share_kernel(*refs):
    share_ref, turned_ref = refs[4:]
    rows = refs[0].shape[1]
    for h in range(2):
        total = refs[2 * h][0] + refs[2 * h + 1][0].astype(jnp.float32)
        share_ref[h * rows : (h + 1) * rows, :] = total.astype(jnp.bfloat16)
    turned_ref[...] = share_ref[...].T


def finish_share(pieces, others):
    _, rows, width = pieces[0][1].shape
    return pl.pallas_call(
        share_kernel,
        out_shape=[
            jax.ShapeDtypeStruct((2 * rows, width), jnp.bfloat16),
            jax.ShapeDtypeStruct((width, 2 * rows), jnp.bfloat16),
        ],
        compiler_params=pltpu.CompilerParams(vmem_limit_bytes=24 * MIB),
        cost_estimate=pl.CostEstimate(
            flops=0, bytes_accessed=20 * rows * width, transcendentals=0
        ),
        name="share",
    )(pieces[0][1], others[0], pieces[1][1], others[1])


def sum_over_rows(xs, weights, order_sent, order_kept, row_partner, beside):
    pieces = pair_products(xs, weights, order_sent, order_kept, row_partner, beside)
    bits = weights.shape[0].bit_length() - 2
    for level in range(bits):
        masks = (2 << level, 1 << (bits - level))
        others = [
            lax.ppermute(sent, "row", row_partner(mask)) for (sent, _), mask in zip(pieces, masks)
        ]
        others = tie(others, beside(level + 1))
        if level < bits - 1:
            pieces = halve(pieces, others)
    share, turned = finish_share(pieces, others)
    return share, turned


def final_kernel(count, places, sub_width, scale, diagonal, with_previous, info_ref, *refs):
    groups = 2 * GROUPS
    lhs = refs[:count]
    rhs = refs[count : count + groups]
    omega_ref, sign_ref, row_ref, col_ref = refs[count + groups : count + groups + 4]
    out_ref, lhs_ref, cross_ref, rate_ref = refs[count + groups + 4 + with_previous :]
    rows = omega_ref.shape[0]
    cross = cross_ref.reshape(rows * SUBS, LANES)
    per_block = sub_width // LANES
    blocks = SUBS // per_block

    @pl.when(pl.program_id(0) == 0)
    def _():
        for k, source, target, size in places:
            lhs_ref[:, target : target + size] = lhs[k][:, source : source + size]
        rate = rate_ref.reshape(rows * SUBS, LANES)
        for c in range(SUBS):
            rate[pl.ds(c, rows, stride=SUBS), :] = jnp.broadcast_to(row_ref[...], (rows, LANES))

    for b in range(blocks):
        right = jnp.concatenate([r[b] for r in rhs], axis=0)
        total = jnp.dot(lhs_ref[...], right, preferred_element_type=jnp.float32)
        for lane in range(0, sub_width, LANES):
            spot = pl.ds(b * per_block + lane // LANES, rows, stride=SUBS)
            cross[spot, :] = total[:, lane : lane + LANES]

    col_rate = col_ref[...][None]
    col_shift = col_rate * PENALTY
    col_smooth = col_rate * scale
    for first in range(0, rows, 64):
        part = slice(first, min(first + 64, rows))
        row_rate = rate_ref[part]
        trial = omega_ref[part] - (row_rate * col_smooth) * cross_ref[part]
        sign = sign_ref[part].astype(jnp.float32)
        out_ref[part] = sign * jnp.maximum(sign * trial - row_rate * col_shift, 0.0)

    if diagonal:
        @pl.when(pl.program_id(0) == info_ref[1] // blocks)
        def _():
            first_tile = info_ref[1] % blocks * per_block
            for first in range(0, rows, 64):
                part = slice(first, min(first + 64, rows))
                shape = out_ref[part].shape
                rate = rate_ref[part] * col_rate
                trial = omega_ref[part] - rate * (cross_ref[part] * scale)
                value = 0.5 * (trial + jnp.sqrt(trial * trial + 4.0 * rate))
                row_ids = lax.broadcasted_iota(jnp.int32, shape, 0) + first
                tile_ids = lax.broadcasted_iota(jnp.int32, shape, 1) - first_tile
                col_ids = tile_ids * LANES + lax.broadcasted_iota(jnp.int32, shape, 2)
                out_ref[part] = jnp.where(row_ids == col_ids, value, out_ref[part])


def final_update(lhs, places, rhs, omega3, sign3, row_rate, col_rate, info, previous, scale):
    row_total, lane_tiles, _ = omega3.shape
    tile = sub_width = rhs[0][0].shape[2]
    depth = sum(size for _, _, _, size in places)
    sample_count = depth // len(rhs)
    blocks = SUBS * LANES // sub_width
    diagonal = previous is None
    grid_block = pl.BlockSpec((tile, SUBS, LANES), lambda j, p: (p[0], j, 0))
    lhs_specs = [
        pl.BlockSpec((tile, a.shape[1]), (lambda j, p: (p[0], 0)) if by_row else (lambda j, p: (0, 0)))
        for a, by_row in lhs
    ]
    rhs_specs = [
        pl.BlockSpec((blocks, sample_count, sub_width), lambda j, p, at=at: (j, at, 0))
        for _, at in rhs
    ]
    operands = [a for a, _ in lhs] + [b for b, _ in rhs] + [omega3, sign3, row_rate, col_rate]
    specs = (
        lhs_specs
        + rhs_specs
        + [
            grid_block,
            grid_block,
            pl.BlockSpec((tile, 1), lambda j, p: (p[0], 0)),
            pl.BlockSpec((SUBS, LANES), lambda j, p: (j, 0)),
        ]
    )
    aliases = {}
    if previous is not None:
        operands.append(previous)
        specs.append(pl.BlockSpec(memory_space=pl.ANY))
        aliases = {len(operands): 0}
    elements = tile * lane_tiles * LANES
    return pl.pallas_call(
        functools.partial(
            final_kernel, len(lhs), places, sub_width, scale, diagonal, previous is not None
        ),
        grid_spec=pltpu.PrefetchScalarGridSpec(
            num_scalar_prefetch=1,
            grid=(lane_tiles // SUBS,),
            in_specs=specs,
            out_specs=grid_block,
            scratch_shapes=[
                pltpu.VMEM((tile, depth), jnp.bfloat16),
                pltpu.VMEM((tile, SUBS, LANES), jnp.float32),
                pltpu.VMEM((tile, SUBS, LANES), jnp.float32),
            ],
        ),
        out_shape=jax.ShapeDtypeStruct(omega3.shape, jnp.float32),
        input_output_aliases=aliases,
        compiler_params=pltpu.CompilerParams(vmem_limit_bytes=56 * MIB),
        cost_estimate=pl.CostEstimate(
            flops=2 * depth * elements, bytes_accessed=elements * 16, transcendentals=0
        ),
        name="final_update",
    )(info, *operands)


def body(samples, omega, sign_mask, step_size):
    row_total, group_count, _, sub_width = omega.shape
    lane_tiles = group_count * sub_width // LANES
    row_count = lax.axis_size("row")
    col_count = lax.axis_size("col")
    row_index = lax.axis_index("row").astype(jnp.int32)
    col_index = lax.axis_index("col").astype(jnp.int32)
    part = samples.shape[0]
    sample_total = part * col_count
    per_group = col_count // GROUPS
    omega3 = omega.reshape(row_total, lane_tiles, LANES)
    sign3 = sign_mask.reshape(row_total, lane_tiles, LANES)

    def row_partner(mask):
        return [(r, r ^ mask) for r in range(row_count)]

    ring = [(c, (c + 1) % col_count) for c in range(col_count)]
    relative = jnp.arange(row_count // 2, dtype=jnp.int32)
    order_kept = ((row_index >> 1) ^ relative) * 2 + (row_index & 1)
    order_sent = order_kept ^ 1

    xs = [[samples[k * part // PIECES : (k + 1) * part // PIECES] for k in range(PIECES)]]
    x_turned, y_rings = [], []
    weights = convert(omega3, group_count, sub_width)

    def advance(entries):
        if isinstance(entries[-1], list):
            if len(entries[-1]) == PIECES:
                entries.append([])
            done = lax.ppermute(entries[-2][len(entries[-1])], "col", ring)
            entries[-1].append(done)
        else:
            entries.append(lax.ppermute(entries[-1], "col", ring))
            done = entries[-1]
        return done

    def complete(length):
        return len(xs) >= length and len(xs[length - 1]) == PIECES

    def gather(rows):
        return lax.all_gather(jnp.concatenate(rows, axis=0), "row", axis=0, tiled=False)

    x_cols, y_cols, waiting = [], [], []
    for k in range(GROUPS):
        first = k * per_group
        while not complete(first + per_group):
            advance(xs)
        if not k:
            xs[-1] = tie(xs[-1], [weights])
        group = xs[first : first + per_group]
        own = [
            lax.dynamic_slice_in_dim(x, col_index * sub_width, sub_width, 1)
            for pieces in group
            for x in pieces
        ]
        block = gather(own + waiting)
        x_cols.append((block, 0))
        if waiting:
            y_cols.append((block, 1))

        def beside(exchange):
            done = []
            if exchange == 0:
                x_turned.extend(turn(x, sub_width) for x in group)
                done.extend(x_turned[first:])
                done.extend(block for block, _ in x_cols[:-1])
            for _ in range(X_STEPS[min(exchange, len(X_STEPS) - 1)]):
                if not complete(col_count):
                    done.append(advance(xs))
            if y_rings and len(y_rings[0]) < col_count:
                done.append(advance(y_rings[0]))
            return done

        share, turned = sum_over_rows(
            [x for pieces in group for x in pieces],
            weights,
            order_sent,
            order_kept,
            row_partner,
            beside,
        )
        waiting = [share]
        y_rings.append([turned])
    last = gather(tie(waiting, [x_cols[-1][0]]))
    for pieces in y_rings:
        while len(pieces) < col_count:
            advance(pieces)
    last = tie(last, [pieces[-2] for pieces in y_rings])
    y_cols.append((last, 0))
    group_rows = part * per_group

    def mean_square(pieces, axis):
        total = sum(jnp.sum(jnp.square(p.astype(jnp.float32)), axis=axis) for p in pieces)
        total = lax.optimization_barrier(total) / sample_total + 1e-06
        return lax.optimization_barrier(total.astype(jnp.bfloat16)).astype(jnp.float32)

    x_pieces = [x for pieces in xs for x in pieces]
    row_rate = (step_size[0] * lax.rsqrt(mean_square(x_pieces, 0)))[:, None]
    col_rate = lax.rsqrt(mean_square([block[:, :group_rows] for block, _ in x_cols], 1))
    col_rate = col_rate.reshape(lane_tiles, LANES)
    x_places = tuple((s, 0, s * part, part) for s in range(col_count))

    updated = None
    for distance in range(col_count):
        y_places = tuple(
            (
                col_count + s // per_group,
                s % per_group * part,
                sample_total + (s + distance) % col_count * part,
                part,
            )
            for s in range(col_count)
        )
        lhs = [(x, True) for x in x_turned] + [(y[distance], False) for y in y_rings]
        info = jnp.stack([(col_index - distance + col_count) % col_count, row_index])
        updated = final_update(
            lhs,
            x_places + y_places,
            y_cols + x_cols,
            omega3,
            sign3,
            row_rate,
            col_rate,
            info,
            updated,
            0.5 / sample_total,
        )
    return updated.reshape(omega.shape)


def solution(mesh):
    in_specs = (P("col", "row"), P("row", None, "col", None), P("row", None, "col", None), P())
    out_specs = P("row", None, "col", None)
    return jax.shard_map(body, mesh=mesh, in_specs=in_specs, out_specs=out_specs, check_vma=False)
```

```python
import functools

import jax
import jax.numpy as jnp
from jax import lax
from jax.experimental import pallas as pl
from jax.experimental.pallas import tpu as pltpu
from jax.sharding import PartitionSpec as P

PENALTY = 0.05
LANES = 128
SUBS = 8
GROUPS = 2
PIECES = 2
X_STEPS = (1, 2, 1)
Y_STEPS = (0, 2, 0)
MIB = 1 << 20


def convert_kernel(omega_ref, out_ref):
    rows = omega_ref.shape[0]
    blocks, _, width = out_ref.shape
    flat = omega_ref.reshape(rows * SUBS, LANES)
    per_block = width // LANES
    for c in range(SUBS):
        piece = flat[pl.ds(c, rows, stride=SUBS), :].astype(jnp.bfloat16)
        lane = (c % per_block) * LANES
        out_ref[c // per_block, :, lane : lane + LANES] = piece


def convert(omega3, group_count, sub_width):
    row_total, lane_tiles, _ = omega3.shape
    tile = min(512, row_total)
    blocks = SUBS * LANES // sub_width
    return pl.pallas_call(
        convert_kernel,
        grid=(row_total // tile, lane_tiles // SUBS),
        in_specs=[pl.BlockSpec((tile, SUBS, LANES), lambda i, j: (i, j, 0))],
        out_specs=pl.BlockSpec((blocks, tile, sub_width), lambda i, j: (j, i, 0)),
        out_shape=jax.ShapeDtypeStruct((group_count, row_total, sub_width), jnp.bfloat16),
        compiler_params=pltpu.CompilerParams(vmem_limit_bytes=32 * MIB),
        cost_estimate=pl.CostEstimate(flops=0, bytes_accessed=omega3.size * 6, transcendentals=0),
        name="omega_to_bf16",
    )(omega3)


def turn_kernel(*refs):
    refs[-1][...] = jnp.concatenate([r[...] for r in refs[:-1]], axis=0).T


def turn(pieces, width):
    rows, total = pieces[0].shape
    count = rows * len(pieces)
    return pl.pallas_call(
        turn_kernel,
        grid=(total // width,),
        in_specs=[pl.BlockSpec((rows, width), lambda i: (0, i)) for _ in pieces],
        out_specs=pl.BlockSpec((width, count), lambda i: (i, 0)),
        out_shape=jax.ShapeDtypeStruct((total, count), pieces[0].dtype),
        compiler_params=pltpu.CompilerParams(vmem_limit_bytes=16 * MIB),
        cost_estimate=pl.CostEstimate(
            flops=0, bytes_accessed=4 * count * total, transcendentals=0
        ),
        name="turn",
    )(*pieces)


def tie(values, done):
    return lax.optimization_barrier((values, done))[0] if done else values


def multiply_rows(x_refs, weight):
    rows = jnp.concatenate([x[...] for x in x_refs], axis=0)
    return jnp.dot(rows, weight, preferred_element_type=jnp.float32)


def sent_kernel(count, order_ref, *refs):
    x_refs, w_ref, out_ref = refs[:count], refs[count], refs[count + 1]
    rows = jnp.concatenate([x[...] for x in x_refs], axis=0)
    step = min(256, rows.shape[0])
    for first in range(0, rows.shape[0], step):
        piece = jnp.dot(
            rows[first : first + step], w_ref[0], preferred_element_type=jnp.float32
        )
        out_ref[0, first : first + step, :] = piece.astype(jnp.bfloat16)


def reversed_bits(value, bits):
    return sum(((value >> b) & 1) << (bits - 1 - b) for b in range(bits))


def kept_kernel(count, bits, order_ref, *refs):
    x_refs, w_ref, other_ref = refs[:count], refs[count], refs[count + 1]
    halves = (refs[count + 2 : count + 4], refs[count + 4 : count + 6])
    total = multiply_rows(x_refs, w_ref[0]) + other_ref[0].astype(jnp.float32)
    rows = total.shape[0] // 2
    step = pl.program_id(0)
    split = 1 << (bits - 1)
    for relative in range(1 << bits):

        @pl.when(step == relative)
        def _():
            for h, (sent_ref, kept_ref) in enumerate(halves):
                place = relative if h else reversed_bits(relative, bits)
                target = sent_ref if place >= split else kept_ref
                target[place % split] = total[h * rows : (h + 1) * rows].astype(target.dtype)


def pair_products(xs, weights, order_sent, order_kept, row_partner, beside):
    count = len(xs)
    rows, depth = xs[0].shape
    group_count, _, width = weights.shape
    blocks = group_count // 2
    bits = blocks.bit_length() - 1
    total_rows = count * rows
    x_spec = pl.BlockSpec((rows, depth), lambda g, order: (0, 0))
    w_spec = pl.BlockSpec((1, depth, width), lambda g, order: (order[g], 0, 0))
    block_spec = pl.BlockSpec((1, total_rows, width), lambda g, order: (g, 0, 0))
    cost = pl.CostEstimate(
        flops=2 * total_rows * depth * blocks * width,
        bytes_accessed=weights.size + 2 * count * xs[0].size + 2 * blocks * total_rows * width,
        transcendentals=0,
    )
    params = pltpu.CompilerParams(vmem_limit_bytes=48 * MIB)
    sent = pl.pallas_call(
        functools.partial(sent_kernel, count),
        grid_spec=pltpu.PrefetchScalarGridSpec(
            num_scalar_prefetch=1,
            grid=(blocks,),
            in_specs=[x_spec] * count + [w_spec],
            out_specs=block_spec,
        ),
        out_shape=jax.ShapeDtypeStruct((blocks, total_rows, width), jnp.bfloat16),
        compiler_params=params,
        cost_estimate=cost,
        name="products_sent",
    )(order_sent, *xs, weights)
    other = tie(lax.ppermute(sent, "row", row_partner(1)), beside(0, sent))
    half = (blocks // 2, total_rows // 2, width)
    half_spec = pl.BlockSpec(half, lambda g, order: (0, 0, 0))
    outs = pl.pallas_call(
        functools.partial(kept_kernel, count, bits),
        grid_spec=pltpu.PrefetchScalarGridSpec(
            num_scalar_prefetch=1,
            grid=(blocks,),
            in_specs=[x_spec] * count + [w_spec, block_spec],
            out_specs=[half_spec] * 4,
        ),
        out_shape=[
            jax.ShapeDtypeStruct(half, jnp.bfloat16),
            jax.ShapeDtypeStruct(half, jnp.float32),
        ]
        * 2,
        compiler_params=params,
        cost_estimate=cost,
        name="products_kept",
    )(order_kept, *xs, weights, other)
    return [(outs[0], outs[1]), (outs[2], outs[3])]


def halve_kernel(split, *refs):
    for h in range(2):
        kept_ref, other_ref, next_sent, next_kept = refs[2 * h], refs[2 * h + 1], refs[4 + 2 * h], refs[5 + 2 * h]
        next_kept[...] = kept_ref[:split] + other_ref[:split].astype(jnp.float32)
        total = kept_ref[split:] + other_ref[split:].astype(jnp.float32)
        next_sent[...] = total.astype(jnp.bfloat16)


def halve(pieces, others):
    kept = pieces[0][1]
    split = kept.shape[0] // 2
    shape = (split,) + kept.shape[1:]
    outs = pl.pallas_call(
        functools.partial(halve_kernel, split),
        out_shape=[
            jax.ShapeDtypeStruct(shape, jnp.bfloat16),
            jax.ShapeDtypeStruct(shape, jnp.float32),
        ]
        * 2,
        compiler_params=pltpu.CompilerParams(vmem_limit_bytes=32 * MIB),
        cost_estimate=pl.CostEstimate(flops=0, bytes_accessed=18 * kept.size, transcendentals=0),
        name="halve",
    )(pieces[0][1], others[0], pieces[1][1], others[1])
    return [(outs[0], outs[1]), (outs[2], outs[3])]


def share_kernel(*refs):
    share_ref, turned_ref = refs[4:]
    rows = refs[0].shape[1]
    for h in range(2):
        total = refs[2 * h][0] + refs[2 * h + 1][0].astype(jnp.float32)
        share_ref[h * rows : (h + 1) * rows, :] = total.astype(jnp.bfloat16)
    turned_ref[...] = share_ref[...].T


def finish_share(pieces, others):
    _, rows, width = pieces[0][1].shape
    return pl.pallas_call(
        share_kernel,
        out_shape=[
            jax.ShapeDtypeStruct((2 * rows, width), jnp.bfloat16),
            jax.ShapeDtypeStruct((width, 2 * rows), jnp.bfloat16),
        ],
        compiler_params=pltpu.CompilerParams(vmem_limit_bytes=24 * MIB),
        cost_estimate=pl.CostEstimate(
            flops=0, bytes_accessed=20 * rows * width, transcendentals=0
        ),
        name="share",
    )(pieces[0][1], others[0], pieces[1][1], others[1])


def sum_over_rows(xs, weights, order_sent, order_kept, row_partner, beside):
    pieces = pair_products(xs, weights, order_sent, order_kept, row_partner, beside)
    bits = weights.shape[0].bit_length() - 2
    for level in range(bits):
        masks = (2 << level, 1 << (bits - level))
        others = [
            lax.ppermute(sent, "row", row_partner(mask)) for (sent, _), mask in zip(pieces, masks)
        ]
        others = tie(others, beside(level + 1, pieces[0][0]))
        if level < bits - 1:
            pieces = halve(pieces, others)
    share, turned = finish_share(pieces, others)
    return share, turned


def final_kernel(x_count, y_count, y_places, sub_width, scale, info_ref, *refs):
    xs, refs = refs[:x_count], refs[x_count:]
    ys, refs = refs[:y_count], refs[y_count:]
    rhs, refs = refs[: 2 * x_count], refs[2 * x_count :]
    omega_ref, sign_ref, row_ref, col_ref, out_ref, lhs_ref, cross_ref = refs
    rows = omega_ref.shape[0]
    cross = cross_ref.reshape(rows * SUBS, LANES)
    per_block = sub_width // LANES
    blocks = SUBS // per_block
    distance = pl.program_id(1)
    part = xs[0].shape[1]
    for k, x in enumerate(xs):
        lhs_ref[:, k * part : (k + 1) * part] = x[...]
    for value, places in enumerate(y_places):

        @pl.when(distance == value)
        def _():
            for k, source, target in places:
                lhs_ref[:, target : target + part] = ys[k][:, source : source + part]

    for b in range(blocks):
        right = jnp.concatenate([r[b] for r in rhs], axis=0)
        total = jnp.dot(lhs_ref[...], right, preferred_element_type=jnp.float32)
        for lane in range(0, sub_width, LANES):
            spot = pl.ds(b * per_block + lane // LANES, rows, stride=SUBS)
            cross[spot, :] = total[:, lane : lane + LANES]

    col_rate = col_ref[...][None]
    col_shift = col_rate * PENALTY
    col_smooth = col_rate * scale
    for first in range(0, rows, 64):
        span = slice(first, min(first + 64, rows))
        row_rate = row_ref[span]
        trial = omega_ref[span] - (row_rate * col_smooth) * cross_ref[span]
        sign = sign_ref[span].astype(jnp.float32)
        out_ref[span] = sign * jnp.maximum(sign * trial - row_rate * col_shift, 0.0)

    @pl.when(jnp.logical_and(distance == 0, pl.program_id(0) == info_ref[0] // blocks))
    def _():
        first_tile = info_ref[0] % blocks * per_block
        for first in range(0, rows, 64):
            span = slice(first, min(first + 64, rows))
            shape = out_ref[span].shape
            rate = row_ref[span] * col_rate
            trial = omega_ref[span] - rate * (cross_ref[span] * scale)
            value = 0.5 * (trial + jnp.sqrt(trial * trial + 4.0 * rate))
            row_ids = lax.broadcasted_iota(jnp.int32, shape, 0) + first
            tile_ids = lax.broadcasted_iota(jnp.int32, shape, 1) - first_tile
            col_ids = tile_ids * LANES + lax.broadcasted_iota(jnp.int32, shape, 2)
            out_ref[span] = jnp.where(row_ids == col_ids, value, out_ref[span])


def final_update(xs, ys, y_places, rhs, omega3, sign3, row_rate, col_rate, info, scale):
    row_total, lane_tiles, _ = omega3.shape
    part = xs[0].shape[1]
    tile = sub_width = rhs[0][0].shape[2]
    blocks = SUBS * LANES // sub_width
    depth = part * len(rhs)
    grid_block = pl.BlockSpec((tile, SUBS, LANES), lambda j, d, p: (p[1 + d], j, 0))
    return pl.pallas_call(
        functools.partial(final_kernel, len(xs), len(ys), y_places, sub_width, scale),
        grid_spec=pltpu.PrefetchScalarGridSpec(
            num_scalar_prefetch=1,
            grid=(lane_tiles // SUBS, row_total // tile),
            in_specs=[pl.BlockSpec((tile, part), lambda j, d, p: (p[1 + d], 0)) for _ in xs]
            + [pl.BlockSpec(y.shape, lambda j, d, p: (0, 0)) for y in ys]
            + [
                pl.BlockSpec((blocks, part, sub_width), lambda j, d, p, at=at: (j, at, 0))
                for _, at in rhs
            ]
            + [
                grid_block,
                grid_block,
                pl.BlockSpec((tile, SUBS, LANES), lambda j, d, p: (p[1 + d], 0, 0)),
                pl.BlockSpec((SUBS, LANES), lambda j, d, p: (j, 0)),
            ],
            out_specs=grid_block,
            scratch_shapes=[
                pltpu.VMEM((tile, depth), jnp.bfloat16),
                pltpu.VMEM((tile, SUBS, LANES), jnp.float32),
            ],
        ),
        out_shape=jax.ShapeDtypeStruct(omega3.shape, jnp.float32),
        compiler_params=pltpu.CompilerParams(vmem_limit_bytes=56 * MIB),
        cost_estimate=pl.CostEstimate(
            flops=2 * depth * omega3.size, bytes_accessed=omega3.size * 16, transcendentals=0
        ),
        name="final_update",
    )(info, *xs, *ys, *[b for b, _ in rhs], omega3, sign3, row_rate, col_rate)


def body(samples, omega, sign_mask, step_size):
    row_total, group_count, _, sub_width = omega.shape
    lane_tiles = group_count * sub_width // LANES
    row_count = lax.axis_size("row")
    col_count = lax.axis_size("col")
    row_index = lax.axis_index("row").astype(jnp.int32)
    col_index = lax.axis_index("col").astype(jnp.int32)
    part = samples.shape[0]
    sample_total = part * col_count
    per_group = col_count // GROUPS
    omega3 = omega.reshape(row_total, lane_tiles, LANES)
    sign3 = sign_mask.reshape(row_total, lane_tiles, LANES)

    def row_partner(mask):
        return [(r, r ^ mask) for r in range(row_count)]

    ring = [(c, (c + 1) % col_count) for c in range(col_count)]
    relative = jnp.arange(row_count // 2, dtype=jnp.int32)
    order_kept = ((row_index >> 1) ^ relative) * 2 + (row_index & 1)
    order_sent = order_kept ^ 1

    xs = [[samples[k * part // PIECES : (k + 1) * part // PIECES] for k in range(PIECES)]]
    x_turned, y_rings = [], []
    weights = convert(omega3, group_count, sub_width)

    def advance(entries, after=()):
        if isinstance(entries[-1], list):
            if len(entries[-1]) == PIECES:
                entries.append([])
            done = tie(lax.ppermute(entries[-2][len(entries[-1])], "col", ring), after)
            entries[-1].append(done)
        else:
            entries.append(tie(lax.ppermute(entries[-1], "col", ring), after))
            done = entries[-1]
        return done

    def complete(length):
        return len(xs) >= length and len(xs[length - 1]) == PIECES

    def gather(rows):
        return lax.all_gather(jnp.concatenate(rows, axis=0), "row", axis=0, tiled=False)

    x_cols, y_cols, blocks, waiting, marks = [], [], [], [], []

    def gather(pieces_list, shares):
        own = [
            lax.dynamic_slice_in_dim(x, col_index * sub_width, sub_width, 1)
            for pieces in pieces_list
            for x in pieces
        ]
        block = lax.all_gather(jnp.concatenate(own + shares, axis=0), "row", axis=0, tiled=False)
        count = len(pieces_list)
        x_cols.extend((block, k) for k in range(count))
        y_cols.extend((block, count + k) for k in range(per_group * len(shares)))
        blocks.append(block)

    for k in range(GROUPS):
        first = k * per_group
        while not complete(first + per_group):
            advance(xs)
        if not k:
            xs[-1] = tie(xs[-1], [weights])
        group = xs[first : first + per_group]
        if k:
            gather([tie(pieces, [marks[1]]) for pieces in group[:-1]], [])
            gather(group[-1:], waiting)
        else:
            gather(group, [])

        def beside(exchange, sent):
            done = []
            marks.append(sent)
            if exchange == 0:
                x_turned.extend(turn(x, sub_width) for x in group)
                done.extend(x_turned[first:])
                done.extend(blocks[:-1])
            for _ in range(X_STEPS[min(exchange, len(X_STEPS) - 1)]):
                if not complete(col_count):
                    done.append(advance(xs, [sent]))
            for _ in range(Y_STEPS[min(exchange, len(Y_STEPS) - 1)]):
                if y_rings and len(y_rings[0]) < col_count:
                    done.append(advance(y_rings[0], [sent]))
            return done

        share, turned = sum_over_rows(
            [x for pieces in group for x in pieces],
            weights,
            order_sent,
            order_kept,
            row_partner,
            beside,
        )
        waiting = [share]
        y_rings.append([turned])
    gather([], tie(waiting, [blocks[-1]]))
    for pieces in y_rings:
        while len(pieces) < col_count:
            advance(pieces)

    def mean_square(pieces, axis):
        total = sum(jnp.sum(jnp.square(p.astype(jnp.float32)), axis=axis) for p in pieces)
        total = lax.optimization_barrier(total) / sample_total + 1e-06
        return lax.optimization_barrier(total.astype(jnp.bfloat16)).astype(jnp.float32)

    x_pieces = [x for pieces in xs for x in pieces]
    row_rate = (step_size[0] * lax.rsqrt(mean_square(x_pieces, 0)))
    row_rate = jnp.broadcast_to(row_rate[:, None, None], (row_total, SUBS, LANES))
    x_blocks = [blocks[0], blocks[1], blocks[2][:, :part]]
    col_rate = lax.rsqrt(mean_square(x_blocks, 1)).reshape(lane_tiles, LANES)

    ys = [y for ring_pieces in y_rings for y in ring_pieces]
    y_places = tuple(
        tuple(
            (
                s // per_group * col_count + distance,
                s % per_group * part,
                sample_total + (s + distance) % col_count * part,
            )
            for s in range(col_count)
        )
        for distance in range(col_count)
    )
    planes = (col_index - jnp.arange(col_count, dtype=jnp.int32) + col_count) % col_count
    info = jnp.concatenate([row_index[None], planes])
    updated = final_update(
        x_turned,
        ys,
        y_places,
        y_cols + x_cols,
        omega3,
        sign3,
        row_rate,
        col_rate,
        info,
        0.5 / sample_total,
    )
    return updated.reshape(omega.shape)


def solution(mesh):
    in_specs = (P("col", "row"), P("row", None, "col", None), P("row", None, "col", None), P())
    out_specs = P("row", None, "col", None)
    return jax.shard_map(body, mesh=mesh, in_specs=in_specs, out_specs=out_specs, check_vma=False)
```

```python
import functools

import jax
import jax.numpy as jnp
from jax import lax
from jax.experimental import pallas as pl
from jax.experimental.pallas import tpu as pltpu
from jax.sharding import PartitionSpec as P

PENALTY = 0.05
LANES = 128
SUBS = 8
GROUPS = 2
PIECES = 2
X_STEPS = (1, 2, 1)
MIB = 1 << 20


def convert_kernel(omega_ref, out_ref):
    rows = omega_ref.shape[0]
    blocks, _, width = out_ref.shape
    flat = omega_ref.reshape(rows * SUBS, LANES)
    per_block = width // LANES
    for c in range(SUBS):
        piece = flat[pl.ds(c, rows, stride=SUBS), :].astype(jnp.bfloat16)
        lane = (c % per_block) * LANES
        out_ref[c // per_block, :, lane : lane + LANES] = piece


def convert(omega3, group_count, sub_width):
    row_total, lane_tiles, _ = omega3.shape
    tile = min(512, row_total)
    blocks = SUBS * LANES // sub_width
    return pl.pallas_call(
        convert_kernel,
        grid=(row_total // tile, lane_tiles // SUBS),
        in_specs=[pl.BlockSpec((tile, SUBS, LANES), lambda i, j: (i, j, 0))],
        out_specs=pl.BlockSpec((blocks, tile, sub_width), lambda i, j: (j, i, 0)),
        out_shape=jax.ShapeDtypeStruct((group_count, row_total, sub_width), jnp.bfloat16),
        compiler_params=pltpu.CompilerParams(vmem_limit_bytes=32 * MIB),
        cost_estimate=pl.CostEstimate(flops=0, bytes_accessed=omega3.size * 6, transcendentals=0),
        name="omega_to_bf16",
    )(omega3)


def turn_kernel(*refs):
    refs[-1][...] = jnp.concatenate([r[...] for r in refs[:-1]], axis=0).T


def turn(pieces, width):
    rows, total = pieces[0].shape
    count = rows * len(pieces)
    return pl.pallas_call(
        turn_kernel,
        grid=(total // width,),
        in_specs=[pl.BlockSpec((rows, width), lambda i: (0, i)) for _ in pieces],
        out_specs=pl.BlockSpec((width, count), lambda i: (i, 0)),
        out_shape=jax.ShapeDtypeStruct((total, count), pieces[0].dtype),
        compiler_params=pltpu.CompilerParams(vmem_limit_bytes=16 * MIB),
        cost_estimate=pl.CostEstimate(
            flops=0, bytes_accessed=4 * count * total, transcendentals=0
        ),
        name="turn",
    )(*pieces)


def tie(values, done):
    return lax.optimization_barrier((values, done))[0] if done else values


def multiply_rows(x_refs, weight):
    rows = jnp.concatenate([x[...] for x in x_refs], axis=0)
    return jnp.dot(rows, weight, preferred_element_type=jnp.float32)


def sent_kernel(count, order_ref, *refs):
    x_refs, w_ref, out_ref = refs[:count], refs[count], refs[count + 1]
    out_ref[0] = multiply_rows(x_refs, w_ref[0]).astype(jnp.bfloat16)


def reversed_bits(value, bits):
    return sum(((value >> b) & 1) << (bits - 1 - b) for b in range(bits))


def kept_kernel(count, bits, order_ref, *refs):
    x_refs, w_ref, other_ref = refs[:count], refs[count], refs[count + 1]
    halves = (refs[count + 2 : count + 4], refs[count + 4 : count + 6])
    total = multiply_rows(x_refs, w_ref[0]) + other_ref[0].astype(jnp.float32)
    rows = total.shape[0] // 2
    step = pl.program_id(0)
    split = 1 << (bits - 1)
    for relative in range(1 << bits):

        @pl.when(step == relative)
        def _():
            for h, (sent_ref, kept_ref) in enumerate(halves):
                place = relative if h else reversed_bits(relative, bits)
                target = sent_ref if place >= split else kept_ref
                target[place % split] = total[h * rows : (h + 1) * rows].astype(target.dtype)


def pair_products(xs, weights, order_sent, order_kept, row_partner, beside):
    count = len(xs)
    rows, depth = xs[0].shape
    group_count, _, width = weights.shape
    blocks = group_count // 2
    bits = blocks.bit_length() - 1
    total_rows = count * rows
    x_spec = pl.BlockSpec((rows, depth), lambda g, order: (0, 0))
    w_spec = pl.BlockSpec((1, depth, width), lambda g, order: (order[g], 0, 0))
    block_spec = pl.BlockSpec((1, total_rows, width), lambda g, order: (g, 0, 0))
    cost = pl.CostEstimate(
        flops=2 * total_rows * depth * blocks * width,
        bytes_accessed=weights.size + 2 * count * xs[0].size + 2 * blocks * total_rows * width,
        transcendentals=0,
    )
    params = pltpu.CompilerParams(vmem_limit_bytes=48 * MIB)
    sent = pl.pallas_call(
        functools.partial(sent_kernel, count),
        grid_spec=pltpu.PrefetchScalarGridSpec(
            num_scalar_prefetch=1,
            grid=(blocks,),
            in_specs=[x_spec] * count + [w_spec],
            out_specs=block_spec,
        ),
        out_shape=jax.ShapeDtypeStruct((blocks, total_rows, width), jnp.bfloat16),
        compiler_params=params,
        cost_estimate=cost,
        name="products_sent",
    )(order_sent, *xs, weights)
    other = tie(lax.ppermute(sent, "row", row_partner(1)), beside(0))
    half = (blocks // 2, total_rows // 2, width)
    half_spec = pl.BlockSpec(half, lambda g, order: (0, 0, 0))
    outs = pl.pallas_call(
        functools.partial(kept_kernel, count, bits),
        grid_spec=pltpu.PrefetchScalarGridSpec(
            num_scalar_prefetch=1,
            grid=(blocks,),
            in_specs=[x_spec] * count + [w_spec, block_spec],
            out_specs=[half_spec] * 4,
        ),
        out_shape=[
            jax.ShapeDtypeStruct(half, jnp.bfloat16),
            jax.ShapeDtypeStruct(half, jnp.float32),
        ]
        * 2,
        compiler_params=params,
        cost_estimate=cost,
        name="products_kept",
    )(order_kept, *xs, weights, other)
    return [(outs[0], outs[1]), (outs[2], outs[3])]


def halve_kernel(split, *refs):
    for h in range(2):
        kept_ref, other_ref, next_sent, next_kept = refs[2 * h], refs[2 * h + 1], refs[4 + 2 * h], refs[5 + 2 * h]
        next_kept[...] = kept_ref[:split] + other_ref[:split].astype(jnp.float32)
        total = kept_ref[split:] + other_ref[split:].astype(jnp.float32)
        next_sent[...] = total.astype(jnp.bfloat16)


def halve(pieces, others):
    kept = pieces[0][1]
    split = kept.shape[0] // 2
    shape = (split,) + kept.shape[1:]
    outs = pl.pallas_call(
        functools.partial(halve_kernel, split),
        out_shape=[
            jax.ShapeDtypeStruct(shape, jnp.bfloat16),
            jax.ShapeDtypeStruct(shape, jnp.float32),
        ]
        * 2,
        compiler_params=pltpu.CompilerParams(vmem_limit_bytes=32 * MIB),
        cost_estimate=pl.CostEstimate(flops=0, bytes_accessed=18 * kept.size, transcendentals=0),
        name="halve",
    )(pieces[0][1], others[0], pieces[1][1], others[1])
    return [(outs[0], outs[1]), (outs[2], outs[3])]


def share_kernel(*refs):
    share_ref, turned_ref = refs[4:]
    rows = refs[0].shape[1]
    for h in range(2):
        total = refs[2 * h][0] + refs[2 * h + 1][0].astype(jnp.float32)
        share_ref[h * rows : (h + 1) * rows, :] = total.astype(jnp.bfloat16)
    turned_ref[...] = share_ref[...].T


def finish_share(pieces, others):
    _, rows, width = pieces[0][1].shape
    return pl.pallas_call(
        share_kernel,
        out_shape=[
            jax.ShapeDtypeStruct((2 * rows, width), jnp.bfloat16),
            jax.ShapeDtypeStruct((width, 2 * rows), jnp.bfloat16),
        ],
        compiler_params=pltpu.CompilerParams(vmem_limit_bytes=24 * MIB),
        cost_estimate=pl.CostEstimate(
            flops=0, bytes_accessed=20 * rows * width, transcendentals=0
        ),
        name="share",
    )(pieces[0][1], others[0], pieces[1][1], others[1])


def sum_over_rows(xs, weights, order_sent, order_kept, row_partner, beside):
    pieces = pair_products(xs, weights, order_sent, order_kept, row_partner, beside)
    bits = weights.shape[0].bit_length() - 2
    for level in range(bits):
        masks = (2 << level, 1 << (bits - level))
        others = [
            lax.ppermute(sent, "row", row_partner(mask)) for (sent, _), mask in zip(pieces, masks)
        ]
        others = tie(others, beside(level + 1))
        if level < bits - 1:
            pieces = halve(pieces, others)
    share, turned = finish_share(pieces, others)
    return share, turned


def update_kernel(sizes, group, sub_width, scale, last, info_ref, *refs):
    col_count, per_group = sizes
    xs, refs = refs[:per_group], refs[per_group:]
    ys, refs = refs[:col_count], refs[col_count:]
    y_cols, refs = refs[:per_group], refs[per_group:]
    x_cols, refs = refs[:col_count], refs[col_count:]
    omega_ref, row_ref, col_ref = refs[:3]
    sign_ref = refs[3] if last else None
    out_ref, cross_ref, rate_ref = refs[3 + last :]
    rows = omega_ref.shape[0]
    cross = cross_ref.reshape(rows * SUBS, LANES)
    per_block = sub_width // LANES
    blocks = SUBS // per_block
    distance = pl.program_id(1)

    @pl.when(pl.program_id(0) == 0)
    def _():
        rate = rate_ref.at[distance].reshape(rows * SUBS, LANES)
        for c in range(SUBS):
            rate[pl.ds(c, rows, stride=SUBS), :] = jnp.broadcast_to(row_ref[...], (rows, LANES))

    for value in range(col_count):

        @pl.when(distance == value)
        def _():
            met = [x_cols[(group * per_group + s + value) % col_count] for s in range(per_group)]
            left = jnp.concatenate([x[...] for x in xs] + [ys[value][...]], axis=1)
            for b in range(blocks):
                right = jnp.concatenate([r[b] for r in (*y_cols, *met)], axis=0)
                total = jnp.dot(left, right, preferred_element_type=jnp.float32)
                for lane in range(0, sub_width, LANES):
                    spot = pl.ds(b * per_block + lane // LANES, rows, stride=SUBS)
                    cross[spot, :] = total[:, lane : lane + LANES]

    col_rate = col_ref[...][None]
    col_shift = col_rate * PENALTY
    col_smooth = col_rate * scale
    for first in range(0, rows, 64):
        span = slice(first, min(first + 64, rows))
        row_rate = rate_ref[distance, span]
        trial = omega_ref[span] - (row_rate * col_smooth) * cross_ref[span]
        if last:
            sign = sign_ref[span].astype(jnp.float32)
            trial = sign * jnp.maximum(sign * trial - row_rate * col_shift, 0.0)
        out_ref[span] = trial

    if last:
        @pl.when(jnp.logical_and(distance == 0, pl.program_id(0) == info_ref[0] // blocks))
        def _():
            first_tile = info_ref[0] % blocks * per_block
            for first in range(0, rows, 64):
                span = slice(first, min(first + 64, rows))
                shape = out_ref[span].shape
                rate = rate_ref[distance, span] * col_rate
                trial = omega_ref[span] - rate * (cross_ref[span] * scale)
                value = 0.5 * (trial + jnp.sqrt(trial * trial + 4.0 * rate))
                row_ids = lax.broadcasted_iota(jnp.int32, shape, 0) + first
                tile_ids = lax.broadcasted_iota(jnp.int32, shape, 1) - first_tile
                col_ids = tile_ids * LANES + lax.broadcasted_iota(jnp.int32, shape, 2)
                out_ref[span] = jnp.where(row_ids == col_ids, value, out_ref[span])


def update(group, xs, ys, y_cols, x_cols, omega3, row_rate, col_rate, sign3, info, scale):
    row_total, lane_tiles, _ = omega3.shape
    part = xs[0].shape[1]
    tile = sub_width = ys[0].shape[0]
    blocks = SUBS * LANES // sub_width
    last = sign3 is not None
    sizes = (len(ys), len(xs))
    grid_block = pl.BlockSpec((tile, SUBS, LANES), lambda j, d, p: (p[1 + d], j, 0))
    columns = list(y_cols) + list(x_cols)
    operands = [*xs, *ys, *[b for b, _ in columns], omega3, row_rate, col_rate]
    return pl.pallas_call(
        functools.partial(update_kernel, sizes, group, sub_width, scale, last),
        grid_spec=pltpu.PrefetchScalarGridSpec(
            num_scalar_prefetch=1,
            grid=(lane_tiles // SUBS, row_total // tile),
            in_specs=[pl.BlockSpec((tile, part), lambda j, d, p: (p[1 + d], 0)) for _ in xs]
            + [pl.BlockSpec(y.shape, lambda j, d, p: (0, 0)) for y in ys]
            + [
                pl.BlockSpec((blocks, part, sub_width), lambda j, d, p, at=at: (j, at, 0))
                for _, at in columns
            ]
            + [
                grid_block,
                pl.BlockSpec((tile, 1), lambda j, d, p: (p[1 + d], 0)),
                pl.BlockSpec((SUBS, LANES), lambda j, d, p: (j, 0)),
            ]
            + [grid_block] * last,
            out_specs=grid_block,
            scratch_shapes=[
                pltpu.VMEM((tile, SUBS, LANES), jnp.float32),
                pltpu.VMEM((row_total // tile, tile, SUBS, LANES), jnp.float32),
            ],
        ),
        out_shape=jax.ShapeDtypeStruct(omega3.shape, jnp.float32),
        compiler_params=pltpu.CompilerParams(vmem_limit_bytes=56 * MIB),
        cost_estimate=pl.CostEstimate(
            flops=4 * part * len(xs) * omega3.size,
            bytes_accessed=omega3.size * 12,
            transcendentals=0,
        ),
        name="last_terms" if last else "first_terms",
    )(info, *operands, *([sign3] if last else []))


def body(samples, omega, sign_mask, step_size):
    row_total, group_count, _, sub_width = omega.shape
    lane_tiles = group_count * sub_width // LANES
    row_count = lax.axis_size("row")
    col_count = lax.axis_size("col")
    row_index = lax.axis_index("row").astype(jnp.int32)
    col_index = lax.axis_index("col").astype(jnp.int32)
    part = samples.shape[0]
    sample_total = part * col_count
    per_group = col_count // GROUPS
    omega3 = omega.reshape(row_total, lane_tiles, LANES)
    sign3 = sign_mask.reshape(row_total, lane_tiles, LANES)

    def row_partner(mask):
        return [(r, r ^ mask) for r in range(row_count)]

    ring = [(c, (c + 1) % col_count) for c in range(col_count)]
    relative = jnp.arange(row_count // 2, dtype=jnp.int32)
    order_kept = ((row_index >> 1) ^ relative) * 2 + (row_index & 1)
    order_sent = order_kept ^ 1

    xs = [[samples[k * part // PIECES : (k + 1) * part // PIECES] for k in range(PIECES)]]
    x_turned, y_planes = [], []
    weights = convert(omega3, group_count, sub_width)

    def advance():
        if len(xs[-1]) == PIECES:
            xs.append([])
        done = lax.ppermute(xs[-2][len(xs[-1])], "col", ring)
        xs[-1].append(done)
        return done

    def to_distance(y, distance):
        if not distance:
            return y
        return lax.ppermute(y, "col", [(c, (c + distance) % col_count) for c in range(col_count)])

    def complete(length):
        return len(xs) >= length and len(xs[length - 1]) == PIECES

    def gather(rows):
        return lax.all_gather(jnp.concatenate(rows, axis=0), "row", axis=0, tiled=False)

    x_cols, y_cols, waiting = [], [], []
    for k in range(GROUPS):
        first = k * per_group
        while not complete(first + per_group):
            advance()
        if not k:
            xs[-1] = tie(xs[-1], [weights])
        group = xs[first : first + per_group]
        own = [
            lax.dynamic_slice_in_dim(x, col_index * sub_width, sub_width, 1)
            for pieces in group
            for x in pieces
        ]
        block = gather(own + waiting)
        x_cols.append((block, 0))
        if waiting:
            y_cols.append((block, 1))

        def beside(exchange):
            done = []
            if exchange == 0:
                x_turned.extend(turn(x, sub_width) for x in group)
                done.extend(x_turned[first:])
                done.extend(block for block, _ in x_cols[:-1])
            for _ in range(X_STEPS[min(exchange, len(X_STEPS) - 1)]):
                if not complete(col_count):
                    done.append(advance())
            if y_planes and exchange == 1:
                done.append(y_planes[0][1])
            if y_planes and exchange == 2:
                done.extend(y_planes[0][2:])
            return done

        share, turned = sum_over_rows(
            [x for pieces in group for x in pieces],
            weights,
            order_sent,
            order_kept,
            row_partner,
            beside,
        )
        waiting = [share]
        y_planes.append([to_distance(turned, distance) for distance in range(col_count)])
    last = gather(tie(waiting, [x_cols[-1][0]]))
    y_cols.append((last, 0))
    group_rows = part * per_group

    def mean_square(pieces, axis):
        total = sum(jnp.sum(jnp.square(p.astype(jnp.float32)), axis=axis) for p in pieces)
        total = lax.optimization_barrier(total) / sample_total + 1e-06
        return lax.optimization_barrier(total.astype(jnp.bfloat16)).astype(jnp.float32)

    x_pieces = [x for pieces in xs for x in pieces]
    row_rate = (step_size[0] * lax.rsqrt(mean_square(x_pieces, 0)))[:, None]
    col_rate = lax.rsqrt(mean_square([block[:, :group_rows] for block, _ in x_cols], 1))
    col_rate = col_rate.reshape(lane_tiles, LANES)

    planes = (col_index - jnp.arange(col_count, dtype=jnp.int32) + col_count) % col_count
    info = jnp.concatenate([row_index[None], planes])
    x_entries = [(block, at * per_group + s) for block, at in x_cols for s in range(per_group)]
    updated = omega3
    for k in range(GROUPS):
        block, at = y_cols[k]
        first = k * per_group
        updated = update(
            k,
            x_turned[first : first + per_group],
            y_planes[k],
            [(block, at * per_group + s) for s in range(per_group)],
            x_entries,
            updated,
            row_rate,
            col_rate,
            sign3 if k == GROUPS - 1 else None,
            info,
            0.5 / sample_total,
        )
    return updated.reshape(omega.shape)


def solution(mesh):
    in_specs = (P("col", "row"), P("row", None, "col", None), P("row", None, "col", None), P())
    out_specs = P("row", None, "col", None)
    return jax.shard_map(body, mesh=mesh, in_specs=in_specs, out_specs=out_specs, check_vma=False)
```

```python
import functools

import jax
import jax.numpy as jnp
from jax import lax
from jax.experimental import pallas as pl
from jax.experimental.pallas import tpu as pltpu
from jax.sharding import PartitionSpec as P

PENALTY = 0.05
LANES = 128
SUBS = 8
GROUPS = 2
PIECES = 2
X_STEPS = (1, 2, 1)
MIB = 1 << 20


def convert_kernel(omega_ref, out_ref):
    rows = omega_ref.shape[0]
    blocks, _, width = out_ref.shape
    flat = omega_ref.reshape(rows * SUBS, LANES)
    per_block = width // LANES
    for c in range(SUBS):
        piece = flat[pl.ds(c, rows, stride=SUBS), :].astype(jnp.bfloat16)
        lane = (c % per_block) * LANES
        out_ref[c // per_block, :, lane : lane + LANES] = piece


def convert(omega3, group_count, sub_width):
    row_total, lane_tiles, _ = omega3.shape
    tile = min(512, row_total)
    blocks = SUBS * LANES // sub_width
    return pl.pallas_call(
        convert_kernel,
        grid=(row_total // tile, lane_tiles // SUBS),
        in_specs=[pl.BlockSpec((tile, SUBS, LANES), lambda i, j: (i, j, 0))],
        out_specs=pl.BlockSpec((blocks, tile, sub_width), lambda i, j: (j, i, 0)),
        out_shape=jax.ShapeDtypeStruct((group_count, row_total, sub_width), jnp.bfloat16),
        compiler_params=pltpu.CompilerParams(vmem_limit_bytes=32 * MIB),
        cost_estimate=pl.CostEstimate(flops=0, bytes_accessed=omega3.size * 6, transcendentals=0),
        name="omega_to_bf16",
    )(omega3)


def turn_kernel(*refs):
    refs[-1][...] = jnp.concatenate([r[...] for r in refs[:-1]], axis=0).T


def turn(pieces, width):
    rows, total = pieces[0].shape
    count = rows * len(pieces)
    return pl.pallas_call(
        turn_kernel,
        grid=(total // width,),
        in_specs=[pl.BlockSpec((rows, width), lambda i: (0, i)) for _ in pieces],
        out_specs=pl.BlockSpec((width, count), lambda i: (i, 0)),
        out_shape=jax.ShapeDtypeStruct((total, count), pieces[0].dtype),
        compiler_params=pltpu.CompilerParams(vmem_limit_bytes=16 * MIB),
        cost_estimate=pl.CostEstimate(
            flops=0, bytes_accessed=4 * count * total, transcendentals=0
        ),
        name="turn",
    )(*pieces)


def tie(values, done):
    return lax.optimization_barrier((values, done))[0] if done else values


def multiply_rows(x_refs, weight):
    rows = jnp.concatenate([x[...] for x in x_refs], axis=0)
    return jnp.dot(rows, weight, preferred_element_type=jnp.float32)


def sent_kernel(count, order_ref, *refs):
    x_refs, w_ref, out_ref = refs[:count], refs[count], refs[count + 1]
    out_ref[0] = multiply_rows(x_refs, w_ref[0]).astype(jnp.bfloat16)


def reversed_bits(value, bits):
    return sum(((value >> b) & 1) << (bits - 1 - b) for b in range(bits))


def kept_kernel(count, bits, order_ref, *refs):
    x_refs, w_ref, other_ref = refs[:count], refs[count], refs[count + 1]
    halves = (refs[count + 2 : count + 4], refs[count + 4 : count + 6])
    total = multiply_rows(x_refs, w_ref[0]) + other_ref[0].astype(jnp.float32)
    rows = total.shape[0] // 2
    step = pl.program_id(0)
    split = 1 << (bits - 1)
    for relative in range(1 << bits):

        @pl.when(step == relative)
        def _():
            for h, (sent_ref, kept_ref) in enumerate(halves):
                place = relative if h else reversed_bits(relative, bits)
                target = sent_ref if place >= split else kept_ref
                target[place % split] = total[h * rows : (h + 1) * rows].astype(target.dtype)


def pair_products(xs, weights, order_sent, order_kept, row_partner, beside):
    count = len(xs)
    rows, depth = xs[0].shape
    group_count, _, width = weights.shape
    blocks = group_count // 2
    bits = blocks.bit_length() - 1
    total_rows = count * rows
    x_spec = pl.BlockSpec((rows, depth), lambda g, order: (0, 0))
    w_spec = pl.BlockSpec((1, depth, width), lambda g, order: (order[g], 0, 0))
    block_spec = pl.BlockSpec((1, total_rows, width), lambda g, order: (g, 0, 0))
    cost = pl.CostEstimate(
        flops=2 * total_rows * depth * blocks * width,
        bytes_accessed=weights.size + 2 * count * xs[0].size + 2 * blocks * total_rows * width,
        transcendentals=0,
    )
    params = pltpu.CompilerParams(vmem_limit_bytes=48 * MIB)
    sent = pl.pallas_call(
        functools.partial(sent_kernel, count),
        grid_spec=pltpu.PrefetchScalarGridSpec(
            num_scalar_prefetch=1,
            grid=(blocks,),
            in_specs=[x_spec] * count + [w_spec],
            out_specs=block_spec,
        ),
        out_shape=jax.ShapeDtypeStruct((blocks, total_rows, width), jnp.bfloat16),
        compiler_params=params,
        cost_estimate=cost,
        name="products_sent",
    )(order_sent, *xs, weights)
    other = tie(lax.ppermute(sent, "row", row_partner(1)), beside(0))
    half = (blocks // 2, total_rows // 2, width)
    half_spec = pl.BlockSpec(half, lambda g, order: (0, 0, 0))
    outs = pl.pallas_call(
        functools.partial(kept_kernel, count, bits),
        grid_spec=pltpu.PrefetchScalarGridSpec(
            num_scalar_prefetch=1,
            grid=(blocks,),
            in_specs=[x_spec] * count + [w_spec, block_spec],
            out_specs=[half_spec] * 4,
        ),
        out_shape=[
            jax.ShapeDtypeStruct(half, jnp.bfloat16),
            jax.ShapeDtypeStruct(half, jnp.float32),
        ]
        * 2,
        compiler_params=params,
        cost_estimate=cost,
        name="products_kept",
    )(order_kept, *xs, weights, other)
    return [(outs[0], outs[1]), (outs[2], outs[3])]


def halve_kernel(split, *refs):
    for h in range(2):
        kept_ref, other_ref, next_sent, next_kept = refs[2 * h], refs[2 * h + 1], refs[4 + 2 * h], refs[5 + 2 * h]
        next_kept[...] = kept_ref[:split] + other_ref[:split].astype(jnp.float32)
        total = kept_ref[split:] + other_ref[split:].astype(jnp.float32)
        next_sent[...] = total.astype(jnp.bfloat16)


def halve(pieces, others):
    kept = pieces[0][1]
    split = kept.shape[0] // 2
    shape = (split,) + kept.shape[1:]
    outs = pl.pallas_call(
        functools.partial(halve_kernel, split),
        out_shape=[
            jax.ShapeDtypeStruct(shape, jnp.bfloat16),
            jax.ShapeDtypeStruct(shape, jnp.float32),
        ]
        * 2,
        compiler_params=pltpu.CompilerParams(vmem_limit_bytes=32 * MIB),
        cost_estimate=pl.CostEstimate(flops=0, bytes_accessed=18 * kept.size, transcendentals=0),
        name="halve",
    )(pieces[0][1], others[0], pieces[1][1], others[1])
    return [(outs[0], outs[1]), (outs[2], outs[3])]


def share_kernel(*refs):
    share_ref, turned_ref = refs[4:]
    rows = refs[0].shape[1]
    for h in range(2):
        total = refs[2 * h][0] + refs[2 * h + 1][0].astype(jnp.float32)
        share_ref[h * rows : (h + 1) * rows, :] = total.astype(jnp.bfloat16)
    turned_ref[...] = share_ref[...].T


def finish_share(pieces, others):
    _, rows, width = pieces[0][1].shape
    return pl.pallas_call(
        share_kernel,
        out_shape=[
            jax.ShapeDtypeStruct((2 * rows, width), jnp.bfloat16),
            jax.ShapeDtypeStruct((width, 2 * rows), jnp.bfloat16),
        ],
        compiler_params=pltpu.CompilerParams(vmem_limit_bytes=24 * MIB),
        cost_estimate=pl.CostEstimate(
            flops=0, bytes_accessed=20 * rows * width, transcendentals=0
        ),
        name="share",
    )(pieces[0][1], others[0], pieces[1][1], others[1])


def sum_over_rows(xs, weights, order_sent, order_kept, row_partner, beside):
    pieces = pair_products(xs, weights, order_sent, order_kept, row_partner, beside)
    bits = weights.shape[0].bit_length() - 2
    for level in range(bits):
        masks = (2 << level, 1 << (bits - level))
        others = [
            lax.ppermute(sent, "row", row_partner(mask)) for (sent, _), mask in zip(pieces, masks)
        ]
        others = tie(others, beside(level + 1))
        if level < bits - 1:
            pieces = halve(pieces, others)
    share, turned = finish_share(pieces, others)
    return share, turned


def update_kernel(sizes, group, sub_width, scale, last, info_ref, *refs):
    col_count, per_group = sizes
    xs, refs = refs[:per_group], refs[per_group:]
    ys, refs = refs[:col_count], refs[col_count:]
    y_cols, refs = refs[:per_group], refs[per_group:]
    x_cols, refs = refs[:col_count], refs[col_count:]
    omega_ref, row_ref, col_ref = refs[:3]
    sign_ref = refs[3] if last else None
    out_ref, cross_ref, rate_ref = refs[3 + last :]
    rows = omega_ref.shape[0]
    per_block = sub_width // LANES
    blocks = SUBS // per_block
    width = min(sub_width, 256)
    pieces = [(b, at) for b in range(blocks) for at in range(0, sub_width, width)]
    step = pl.program_id(0)
    ending = step == pl.num_programs(0) - 1
    distance = lax.rem(step, col_count)
    before = jnp.maximum(step - 1, 0)
    old_distance = lax.rem(before, col_count)
    old_tile = lax.div(before, col_count)
    new_cross = cross_ref.at[lax.rem(step, 2)].reshape(rows * SUBS, LANES)
    old_cross = cross_ref.at[lax.rem(step + 1, 2)]

    @pl.when(step < col_count)
    def _():
        rate = rate_ref.at[distance].reshape(rows * SUBS, LANES)
        for c in range(SUBS):
            rate[pl.ds(c, rows, stride=SUBS), :] = jnp.broadcast_to(row_ref[...], (rows, LANES))

    def take_off(first_row, row_count):
        col_rate = col_ref[...][None]
        col_shift = col_rate * PENALTY
        col_smooth = col_rate * scale
        for first in range(first_row, first_row + row_count, 16):
            span = slice(first, min(first + 16, first_row + row_count))
            row_rate = rate_ref[old_distance, span]
            trial = omega_ref[span] - (row_rate * col_smooth) * old_cross[span]
            if last:
                sign = sign_ref[span].astype(jnp.float32)
                trial = sign * jnp.maximum(sign * trial - row_rate * col_shift, 0.0)
            out_ref[span] = trial

    share = rows // len(pieces)
    for value in range(col_count):

        @pl.when(jnp.logical_and(distance == value, jnp.logical_not(ending)))
        def _():
            met = [x_cols[(group * per_group + s + value) % col_count] for s in range(per_group)]
            left = jnp.concatenate([x[...] for x in xs] + [ys[value][...]], axis=1)
            for k, (b, at) in enumerate(pieces):
                right = jnp.concatenate(
                    [r[b, :, at : at + width] for r in (*y_cols, *met)], axis=0
                )
                total = jnp.dot(left, right, preferred_element_type=jnp.float32)
                for lane in range(0, width, LANES):
                    spot = pl.ds(b * per_block + (at + lane) // LANES, rows, stride=SUBS)
                    new_cross[spot, :] = total[:, lane : lane + LANES]
                take_off(k * share, share)

    @pl.when(ending)
    def _():
        take_off(0, rows)

    if last:
        diagonal = jnp.logical_and(old_distance == 0, old_tile == info_ref[0] // blocks)

        @pl.when(jnp.logical_and(diagonal, step > 0))
        def _():
            col_rate = col_ref[...][None]
            first_tile = info_ref[0] % blocks * per_block
            for first in range(0, rows, 16):
                span = slice(first, min(first + 16, rows))
                shape = out_ref[span].shape
                rate = rate_ref[old_distance, span] * col_rate
                trial = omega_ref[span] - rate * (old_cross[span] * scale)
                value = 0.5 * (trial + jnp.sqrt(trial * trial + 4.0 * rate))
                row_ids = lax.broadcasted_iota(jnp.int32, shape, 0) + first
                tile_ids = lax.broadcasted_iota(jnp.int32, shape, 1) - first_tile
                col_ids = tile_ids * LANES + lax.broadcasted_iota(jnp.int32, shape, 2)
                out_ref[span] = jnp.where(row_ids == col_ids, value, out_ref[span])


def update(group, xs, ys, y_cols, x_cols, omega3, row_rate, col_rate, sign3, info, scale):
    row_total, lane_tiles, _ = omega3.shape
    part = xs[0].shape[1]
    tile = sub_width = ys[0].shape[0]
    blocks = SUBS * LANES // sub_width
    last = sign3 is not None
    sizes = (len(ys), len(xs))
    planes = row_total // tile
    total = planes * (lane_tiles // SUBS)

    def new_tile(t):
        t = jnp.minimum(t, total - 1)
        return lax.div(t, planes), lax.rem(t, planes)

    def old_tile(t):
        t = jnp.maximum(t - 1, 0)
        return lax.div(t, planes), lax.rem(t, planes)

    def old_block(t, p):
        j, d = old_tile(t)
        return p[1 + d], j, 0

    def new_rows(t, p):
        return p[1 + new_tile(t)[1]], 0

    grid_block = pl.BlockSpec((tile, SUBS, LANES), old_block)
    columns = list(y_cols) + list(x_cols)
    operands = [*xs, *ys, *[b for b, _ in columns], omega3, row_rate, col_rate]
    return pl.pallas_call(
        functools.partial(update_kernel, sizes, group, sub_width, scale, last),
        grid_spec=pltpu.PrefetchScalarGridSpec(
            num_scalar_prefetch=1,
            grid=(total + 1,),
            in_specs=[pl.BlockSpec((tile, part), new_rows) for _ in xs]
            + [pl.BlockSpec(y.shape, lambda t, p: (0, 0)) for y in ys]
            + [
                pl.BlockSpec(
                    (blocks, part, sub_width), lambda t, p, at=at: (new_tile(t)[0], at, 0)
                )
                for _, at in columns
            ]
            + [
                grid_block,
                pl.BlockSpec((tile, 1), new_rows),
                pl.BlockSpec((SUBS, LANES), lambda t, p: (old_tile(t)[0], 0)),
            ]
            + [grid_block] * last,
            out_specs=grid_block,
            scratch_shapes=[
                pltpu.VMEM((2, tile, SUBS, LANES), jnp.float32),
                pltpu.VMEM((planes, tile, SUBS, LANES), jnp.float32),
            ],
        ),
        out_shape=jax.ShapeDtypeStruct(omega3.shape, jnp.float32),
        compiler_params=pltpu.CompilerParams(vmem_limit_bytes=56 * MIB),
        cost_estimate=pl.CostEstimate(
            flops=4 * part * len(xs) * omega3.size,
            bytes_accessed=omega3.size * 12,
            transcendentals=0,
        ),
        name="last_terms" if last else "first_terms",
    )(info, *operands, *([sign3] if last else []))


def body(samples, omega, sign_mask, step_size):
    row_total, group_count, _, sub_width = omega.shape
    lane_tiles = group_count * sub_width // LANES
    row_count = lax.axis_size("row")
    col_count = lax.axis_size("col")
    row_index = lax.axis_index("row").astype(jnp.int32)
    col_index = lax.axis_index("col").astype(jnp.int32)
    part = samples.shape[0]
    sample_total = part * col_count
    per_group = col_count // GROUPS
    omega3 = omega.reshape(row_total, lane_tiles, LANES)
    sign3 = sign_mask.reshape(row_total, lane_tiles, LANES)

    def row_partner(mask):
        return [(r, r ^ mask) for r in range(row_count)]

    ring = [(c, (c + 1) % col_count) for c in range(col_count)]
    relative = jnp.arange(row_count // 2, dtype=jnp.int32)
    order_kept = ((row_index >> 1) ^ relative) * 2 + (row_index & 1)
    order_sent = order_kept ^ 1

    xs = [[samples[k * part // PIECES : (k + 1) * part // PIECES] for k in range(PIECES)]]
    x_turned, y_planes = [], []
    weights = convert(omega3, group_count, sub_width)

    def advance():
        if len(xs[-1]) == PIECES:
            xs.append([])
        done = lax.ppermute(xs[-2][len(xs[-1])], "col", ring)
        xs[-1].append(done)
        return done

    def to_distance(y, distance):
        if not distance:
            return y
        return lax.ppermute(y, "col", [(c, (c + distance) % col_count) for c in range(col_count)])

    def square_sum(pieces, axis):
        return sum(jnp.sum(jnp.square(p.astype(jnp.float32)), axis=axis) for p in pieces)

    sums = []

    def complete(length):
        return len(xs) >= length and len(xs[length - 1]) == PIECES

    def gather(rows):
        return lax.all_gather(jnp.concatenate(rows, axis=0), "row", axis=0, tiled=False)

    x_cols, y_cols, waiting = [], [], []
    for k in range(GROUPS):
        first = k * per_group
        while not complete(first + per_group):
            advance()
        if not k:
            xs[-1] = tie(xs[-1], [weights])
        group = xs[first : first + per_group]
        own = [
            lax.dynamic_slice_in_dim(x, col_index * sub_width, sub_width, 1)
            for pieces in group
            for x in pieces
        ]
        block = gather(own + waiting)
        x_cols.append((block, 0))
        if waiting:
            y_cols.append((block, 1))

        def beside(exchange):
            done = []
            if exchange == 0:
                x_turned.extend(turn(x, sub_width) for x in group)
                done.extend(x_turned[first:])
                done.extend(block for block, _ in x_cols[:-1])
            for _ in range(X_STEPS[min(exchange, len(X_STEPS) - 1)]):
                if not complete(col_count):
                    done.append(advance())
            if y_planes and exchange == 1:
                done.append(y_planes[0][1])
            if y_planes and exchange == 2:
                done.extend(y_planes[0][2:])
                sums.append(square_sum([x for pieces in xs for x in pieces], 0))
                sums.append(square_sum([x_cols[0][0]], 1))
                done.extend(sums)
            return done

        share, turned = sum_over_rows(
            [x for pieces in group for x in pieces],
            weights,
            order_sent,
            order_kept,
            row_partner,
            beside,
        )
        waiting = [share]
        y_planes.append([to_distance(turned, distance) for distance in range(col_count)])
    last = gather(tie(waiting, [x_cols[-1][0]]))
    y_cols.append((last, 0))
    group_rows = part * per_group

    def scale_of(total):
        total = lax.optimization_barrier(total) / sample_total + 1e-06
        return lax.optimization_barrier(total.astype(jnp.bfloat16)).astype(jnp.float32)

    row_sum, col_sum = sums
    col_sum = col_sum + square_sum([block[:, :group_rows] for block, _ in x_cols[1:]], 1)
    row_rate = (step_size[0] * lax.rsqrt(scale_of(row_sum)))[:, None]
    col_rate = lax.rsqrt(scale_of(col_sum)).reshape(lane_tiles, LANES)

    planes = (col_index - jnp.arange(col_count, dtype=jnp.int32) + col_count) % col_count
    info = jnp.concatenate([row_index[None], planes])
    x_entries = [(block, at * per_group + s) for block, at in x_cols for s in range(per_group)]
    updated = omega3
    for k in range(GROUPS):
        block, at = y_cols[k]
        first = k * per_group
        updated = update(
            k,
            x_turned[first : first + per_group],
            y_planes[k],
            [(block, at * per_group + s) for s in range(per_group)],
            x_entries,
            updated,
            row_rate,
            col_rate,
            sign3 if k == GROUPS - 1 else None,
            info,
            0.5 / sample_total,
        )
    return updated.reshape(omega.shape)


def solution(mesh):
    in_specs = (P("col", "row"), P("row", None, "col", None), P("row", None, "col", None), P())
    out_specs = P("row", None, "col", None)
    return jax.shard_map(body, mesh=mesh, in_specs=in_specs, out_specs=out_specs, check_vma=False)
```

```python
import functools

import jax
import jax.numpy as jnp
from jax import lax
from jax.experimental import pallas as pl
from jax.experimental.pallas import tpu as pltpu
from jax.sharding import PartitionSpec as P

PENALTY = 0.05
LANES = 128
SUBS = 8
GROUPS = 2
PIECES = 2
X_STEPS = (1, 2, 1)
MIB = 1 << 20


def convert_kernel(omega_ref, out_ref):
    rows = omega_ref.shape[0]
    blocks, _, width = out_ref.shape
    flat = omega_ref.reshape(rows * SUBS, LANES)
    per_block = width // LANES
    for c in range(SUBS):
        piece = flat[pl.ds(c, rows, stride=SUBS), :].astype(jnp.bfloat16)
        lane = (c % per_block) * LANES
        out_ref[c // per_block, :, lane : lane + LANES] = piece


def convert(omega3, group_count, sub_width):
    row_total, lane_tiles, _ = omega3.shape
    tile = min(512, row_total)
    blocks = SUBS * LANES // sub_width
    return pl.pallas_call(
        convert_kernel,
        grid=(row_total // tile, lane_tiles // SUBS),
        in_specs=[pl.BlockSpec((tile, SUBS, LANES), lambda i, j: (i, j, 0))],
        out_specs=pl.BlockSpec((blocks, tile, sub_width), lambda i, j: (j, i, 0)),
        out_shape=jax.ShapeDtypeStruct((group_count, row_total, sub_width), jnp.bfloat16),
        compiler_params=pltpu.CompilerParams(vmem_limit_bytes=32 * MIB),
        cost_estimate=pl.CostEstimate(flops=0, bytes_accessed=omega3.size * 6, transcendentals=0),
        name="omega_to_bf16",
    )(omega3)


def turn_kernel(*refs):
    refs[-1][...] = jnp.concatenate([r[...] for r in refs[:-1]], axis=0).T


def turn(pieces, width):
    rows, total = pieces[0].shape
    count = rows * len(pieces)
    return pl.pallas_call(
        turn_kernel,
        grid=(total // width,),
        in_specs=[pl.BlockSpec((rows, width), lambda i: (0, i)) for _ in pieces],
        out_specs=pl.BlockSpec((width, count), lambda i: (i, 0)),
        out_shape=jax.ShapeDtypeStruct((total, count), pieces[0].dtype),
        compiler_params=pltpu.CompilerParams(vmem_limit_bytes=16 * MIB),
        cost_estimate=pl.CostEstimate(
            flops=0, bytes_accessed=4 * count * total, transcendentals=0
        ),
        name="turn",
    )(*pieces)


def tie(values, done):
    return lax.optimization_barrier((values, done))[0] if done else values


def multiply_rows(x_refs, weight):
    rows = jnp.concatenate([x[...] for x in x_refs], axis=0)
    return jnp.dot(rows, weight, preferred_element_type=jnp.float32)


def sent_kernel(count, order_ref, *refs):
    x_refs, w_ref, out_ref = refs[:count], refs[count], refs[count + 1]
    out_ref[0] = multiply_rows(x_refs, w_ref[0]).astype(jnp.bfloat16)


def reversed_bits(value, bits):
    return sum(((value >> b) & 1) << (bits - 1 - b) for b in range(bits))


def kept_kernel(count, bits, order_ref, *refs):
    x_refs, w_ref, other_ref = refs[:count], refs[count], refs[count + 1]
    halves = (refs[count + 2 : count + 4], refs[count + 4 : count + 6])
    total = multiply_rows(x_refs, w_ref[0]) + other_ref[0].astype(jnp.float32)
    rows = total.shape[0] // 2
    step = pl.program_id(0)
    split = 1 << (bits - 1)
    for relative in range(1 << bits):

        @pl.when(step == relative)
        def _():
            for h, (sent_ref, kept_ref) in enumerate(halves):
                place = relative if h else reversed_bits(relative, bits)
                target = sent_ref if place >= split else kept_ref
                target[place % split] = total[h * rows : (h + 1) * rows].astype(target.dtype)


def pair_products(xs, weights, order_sent, order_kept, row_partner, beside):
    count = len(xs)
    rows, depth = xs[0].shape
    group_count, _, width = weights.shape
    blocks = group_count // 2
    bits = blocks.bit_length() - 1
    total_rows = count * rows
    x_spec = pl.BlockSpec((rows, depth), lambda g, order: (0, 0))
    w_spec = pl.BlockSpec((1, depth, width), lambda g, order: (order[g], 0, 0))
    block_spec = pl.BlockSpec((1, total_rows, width), lambda g, order: (g, 0, 0))
    cost = pl.CostEstimate(
        flops=2 * total_rows * depth * blocks * width,
        bytes_accessed=weights.size + 2 * count * xs[0].size + 2 * blocks * total_rows * width,
        transcendentals=0,
    )
    params = pltpu.CompilerParams(vmem_limit_bytes=48 * MIB)
    sent = pl.pallas_call(
        functools.partial(sent_kernel, count),
        grid_spec=pltpu.PrefetchScalarGridSpec(
            num_scalar_prefetch=1,
            grid=(blocks,),
            in_specs=[x_spec] * count + [w_spec],
            out_specs=block_spec,
        ),
        out_shape=jax.ShapeDtypeStruct((blocks, total_rows, width), jnp.bfloat16),
        compiler_params=params,
        cost_estimate=cost,
        name="products_sent",
    )(order_sent, *xs, weights)
    other = tie(lax.ppermute(sent, "row", row_partner(1)), beside(0, sent))
    half = (blocks // 2, total_rows // 2, width)
    half_spec = pl.BlockSpec(half, lambda g, order: (0, 0, 0))
    outs = pl.pallas_call(
        functools.partial(kept_kernel, count, bits),
        grid_spec=pltpu.PrefetchScalarGridSpec(
            num_scalar_prefetch=1,
            grid=(blocks,),
            in_specs=[x_spec] * count + [w_spec, block_spec],
            out_specs=[half_spec] * 4,
        ),
        out_shape=[
            jax.ShapeDtypeStruct(half, jnp.bfloat16),
            jax.ShapeDtypeStruct(half, jnp.float32),
        ]
        * 2,
        compiler_params=params,
        cost_estimate=cost,
        name="products_kept",
    )(order_kept, *xs, weights, other)
    return [(outs[0], outs[1]), (outs[2], outs[3])]


def halve_kernel(split, *refs):
    for h in range(2):
        kept_ref, other_ref, next_sent, next_kept = refs[2 * h], refs[2 * h + 1], refs[4 + 2 * h], refs[5 + 2 * h]
        next_kept[...] = kept_ref[:split] + other_ref[:split].astype(jnp.float32)
        total = kept_ref[split:] + other_ref[split:].astype(jnp.float32)
        next_sent[...] = total.astype(jnp.bfloat16)


def halve(pieces, others):
    kept = pieces[0][1]
    split = kept.shape[0] // 2
    shape = (split,) + kept.shape[1:]
    outs = pl.pallas_call(
        functools.partial(halve_kernel, split),
        out_shape=[
            jax.ShapeDtypeStruct(shape, jnp.bfloat16),
            jax.ShapeDtypeStruct(shape, jnp.float32),
        ]
        * 2,
        compiler_params=pltpu.CompilerParams(vmem_limit_bytes=32 * MIB),
        cost_estimate=pl.CostEstimate(flops=0, bytes_accessed=18 * kept.size, transcendentals=0),
        name="halve",
    )(pieces[0][1], others[0], pieces[1][1], others[1])
    return [(outs[0], outs[1]), (outs[2], outs[3])]


def share_kernel(*refs):
    share_ref, turned_ref = refs[4:]
    rows = refs[0].shape[1]
    for h in range(2):
        total = refs[2 * h][0] + refs[2 * h + 1][0].astype(jnp.float32)
        share_ref[h * rows : (h + 1) * rows, :] = total.astype(jnp.bfloat16)
    turned_ref[...] = share_ref[...].T


def finish_share(pieces, others):
    _, rows, width = pieces[0][1].shape
    return pl.pallas_call(
        share_kernel,
        out_shape=[
            jax.ShapeDtypeStruct((2 * rows, width), jnp.bfloat16),
            jax.ShapeDtypeStruct((width, 2 * rows), jnp.bfloat16),
        ],
        compiler_params=pltpu.CompilerParams(vmem_limit_bytes=24 * MIB),
        cost_estimate=pl.CostEstimate(
            flops=0, bytes_accessed=20 * rows * width, transcendentals=0
        ),
        name="share",
    )(pieces[0][1], others[0], pieces[1][1], others[1])


def sum_over_rows(xs, weights, order_sent, order_kept, row_partner, beside):
    pieces = pair_products(xs, weights, order_sent, order_kept, row_partner, beside)
    bits = weights.shape[0].bit_length() - 2
    for level in range(bits):
        masks = (2 << level, 1 << (bits - level))
        others = [
            lax.ppermute(sent, "row", row_partner(mask)) for (sent, _), mask in zip(pieces, masks)
        ]
        others = tie(others, beside(level + 1, pieces[0][0]))
        if level < bits - 1:
            pieces = halve(pieces, others)
    share, turned = finish_share(pieces, others)
    return share, turned


def narrow_kernel(sign_ref, out_ref):
    rows = sign_ref.shape[0]
    flat = sign_ref.reshape(rows * SUBS, LANES)
    for c in range(SUBS):
        piece = flat[pl.ds(c, rows, stride=SUBS), :]
        out_ref[:, c * LANES : (c + 1) * LANES] = piece.astype(jnp.int8)


def narrow(sign3):
    row_total, lane_tiles, _ = sign3.shape
    tile = min(512, row_total)
    return pl.pallas_call(
        narrow_kernel,
        grid=(row_total // tile, lane_tiles // SUBS),
        in_specs=[pl.BlockSpec((tile, SUBS, LANES), lambda i, j: (i, j, 0))],
        out_specs=pl.BlockSpec((tile, SUBS * LANES), lambda i, j: (i, j)),
        out_shape=jax.ShapeDtypeStruct((row_total, lane_tiles * LANES), jnp.int8),
        compiler_params=pltpu.CompilerParams(vmem_limit_bytes=32 * MIB),
        cost_estimate=pl.CostEstimate(flops=0, bytes_accessed=sign3.size * 5, transcendentals=0),
        name="narrow_signs",
    )(sign3)


def update_kernel(sizes, group, sub_width, scale, last, info_ref, *refs):
    col_count, per_group = sizes
    xs, refs = refs[:per_group], refs[per_group:]
    ys, refs = refs[:col_count], refs[col_count:]
    y_cols, refs = refs[:per_group], refs[per_group:]
    x_cols, refs = refs[:col_count], refs[col_count:]
    old_ref, row_ref, col_ref = refs[:3]
    if last:
        sign_ref, out_ref, cross_ref = refs[3:]
    else:
        out_ref = refs[3]
    rows = row_ref.shape[0]
    per_block = sub_width // LANES
    blocks = SUBS // per_block
    width = min(sub_width, 256)
    distance = pl.program_id(1)
    native = (out_ref if last else old_ref).reshape(rows * SUBS, LANES)
    row_rate = jnp.broadcast_to(row_ref[...], (rows, LANES))
    row_smooth = row_rate * scale
    row_shift = row_rate * PENALTY

    for value in range(col_count):

        @pl.when(distance == value)
        def _():
            met = [x_cols[(group * per_group + s + value) % col_count] for s in range(per_group)]
            left = jnp.concatenate([x[...] for x in xs] + [ys[value][...]], axis=1)
            for first in range(0, SUBS * LANES, width):
                b, at = first // sub_width, first % sub_width
                right = jnp.concatenate(
                    [r[b, :, at : at + width] for r in (*y_cols, *met)], axis=0
                )
                total = jnp.dot(left, right, preferred_element_type=jnp.float32)
                if last and value == 0:
                    cross_ref[:, first : first + width] = total
                for lane in range(0, width, LANES):
                    columns = slice(first + lane, first + lane + LANES)
                    spot = pl.ds((first + lane) // LANES, rows, stride=SUBS)
                    col_rate = col_ref[:, columns]
                    taken = (row_smooth * col_rate) * total[:, lane : lane + LANES]
                    if last:
                        trial = old_ref[:, columns].astype(jnp.float32) - taken
                        sign = sign_ref[:, columns].astype(jnp.float32)
                        shift = row_shift * col_rate
                        native[spot, :] = sign * jnp.maximum(sign * trial - shift, 0.0)
                    else:
                        out_ref[:, columns] = (native[spot, :] - taken).astype(out_ref.dtype)

    if last:
        for b in range(blocks):

            @pl.when(jnp.logical_and(distance == 0, pl.program_id(0) * blocks + b == info_ref[0]))
            def _():
                for lane in range(0, sub_width, LANES):
                    first = b * sub_width + lane
                    columns = slice(first, first + LANES)
                    spot = pl.ds(first // LANES, rows, stride=SUBS)
                    rate = row_rate * col_ref[:, columns]
                    trial = old_ref[:, columns].astype(jnp.float32)
                    trial = trial - rate * (cross_ref[:, columns] * scale)
                    value = 0.5 * (trial + jnp.sqrt(trial * trial + 4.0 * rate))
                    row_ids = lax.broadcasted_iota(jnp.int32, (rows, LANES), 0)
                    col_ids = lax.broadcasted_iota(jnp.int32, (rows, LANES), 1) + lane
                    native[spot, :] = jnp.where(row_ids == col_ids, value, native[spot, :])


def update(group, xs, ys, y_cols, x_cols, old, row_rate, col_rate, signs, info, scale):
    row_total = row_rate.shape[0]
    lane_tiles = col_rate.shape[1] // LANES
    part = xs[0].shape[1]
    tile = sub_width = ys[0].shape[0]
    blocks = SUBS * LANES // sub_width
    last = signs is not None
    sizes = (len(ys), len(xs))
    native_block = pl.BlockSpec((tile, SUBS, LANES), lambda j, d, p: (p[1 + d], j, 0))
    row_block = pl.BlockSpec((tile, SUBS * LANES), lambda j, d, p: (p[1 + d], j))
    columns = list(y_cols) + list(x_cols)
    operands = [*xs, *ys, *[b for b, _ in columns], old, row_rate, col_rate]
    if last:
        result = jax.ShapeDtypeStruct((row_total, lane_tiles, LANES), jnp.float32)
    else:
        result = jax.ShapeDtypeStruct((row_total, lane_tiles * LANES), jnp.bfloat16)
    elements = row_total * lane_tiles * LANES
    return pl.pallas_call(
        functools.partial(update_kernel, sizes, group, sub_width, scale, last),
        grid_spec=pltpu.PrefetchScalarGridSpec(
            num_scalar_prefetch=1,
            grid=(lane_tiles // SUBS, row_total // tile),
            in_specs=[pl.BlockSpec((tile, part), lambda j, d, p: (p[1 + d], 0)) for _ in xs]
            + [pl.BlockSpec(y.shape, lambda j, d, p: (0, 0)) for y in ys]
            + [
                pl.BlockSpec((blocks, part, sub_width), lambda j, d, p, at=at: (j, at, 0))
                for _, at in columns
            ]
            + [
                row_block if last else native_block,
                pl.BlockSpec((tile, 1), lambda j, d, p: (p[1 + d], 0)),
                pl.BlockSpec((1, SUBS * LANES), lambda j, d, p: (0, j)),
            ]
            + [row_block] * last,
            out_specs=native_block if last else row_block,
            scratch_shapes=[pltpu.VMEM((tile, SUBS * LANES), jnp.float32)] * last,
        ),
        out_shape=result,
        compiler_params=pltpu.CompilerParams(vmem_limit_bytes=56 * MIB),
        cost_estimate=pl.CostEstimate(
            flops=4 * part * len(xs) * elements, bytes_accessed=elements * 8, transcendentals=0
        ),
        name="last_terms" if last else "first_terms",
    )(info, *operands, *([signs] if last else []))


def body(samples, omega, sign_mask, step_size):
    row_total, group_count, _, sub_width = omega.shape
    lane_tiles = group_count * sub_width // LANES
    row_count = lax.axis_size("row")
    col_count = lax.axis_size("col")
    row_index = lax.axis_index("row").astype(jnp.int32)
    col_index = lax.axis_index("col").astype(jnp.int32)
    part = samples.shape[0]
    sample_total = part * col_count
    per_group = col_count // GROUPS
    omega3 = omega.reshape(row_total, lane_tiles, LANES)
    sign3 = sign_mask.reshape(row_total, lane_tiles, LANES)

    def row_partner(mask):
        return [(r, r ^ mask) for r in range(row_count)]

    ring = [(c, (c + 1) % col_count) for c in range(col_count)]
    relative = jnp.arange(row_count // 2, dtype=jnp.int32)
    order_kept = ((row_index >> 1) ^ relative) * 2 + (row_index & 1)
    order_sent = order_kept ^ 1

    xs = [[samples[k * part // PIECES : (k + 1) * part // PIECES] for k in range(PIECES)]]
    x_turned, y_planes = [], []
    weights = convert(omega3, group_count, sub_width)

    def advance():
        if len(xs[-1]) == PIECES:
            xs.append([])
        done = lax.ppermute(xs[-2][len(xs[-1])], "col", ring)
        xs[-1].append(done)
        return done

    def to_distance(y, distance):
        if not distance:
            return y
        return lax.ppermute(y, "col", [(c, (c + distance) % col_count) for c in range(col_count)])

    def square_sum(pieces, axis):
        return sum(jnp.sum(jnp.square(p.astype(jnp.float32)), axis=axis) for p in pieces)

    sums, signs = [], []

    def complete(length):
        return len(xs) >= length and len(xs[length - 1]) == PIECES

    def gather(rows):
        return lax.all_gather(jnp.concatenate(rows, axis=0), "row", axis=0, tiled=False)

    x_cols, y_cols, waiting = [], [], []
    for k in range(GROUPS):
        first = k * per_group
        while not complete(first + per_group):
            advance()
        if not k:
            xs[-1] = tie(xs[-1], [weights])
        group = xs[first : first + per_group]
        own = [
            lax.dynamic_slice_in_dim(x, col_index * sub_width, sub_width, 1)
            for pieces in group
            for x in pieces
        ]
        block = gather(own + waiting)
        x_cols.append((block, 0))
        if waiting:
            y_cols.append((block, 1))

        def beside(exchange, sent):
            done = []
            if exchange == 0:
                x_turned.extend(turn(x, sub_width) for x in group)
                done.extend(x_turned[first:])
                done.extend(block for block, _ in x_cols[:-1])
            for _ in range(X_STEPS[min(exchange, len(X_STEPS) - 1)]):
                if not complete(col_count):
                    done.append(advance())
            if y_planes and exchange == 1:
                done.append(y_planes[0][1])
                signs.append(narrow(tie(sign3, [sent])))
                done.extend(signs)
            if y_planes and exchange == 2:
                done.extend(y_planes[0][2:])
                sums.append(square_sum([x for pieces in xs for x in pieces], 0))
                sums.append(square_sum([x_cols[0][0]], 1))
                done.extend(sums)
            return done

        share, turned = sum_over_rows(
            [x for pieces in group for x in pieces],
            weights,
            order_sent,
            order_kept,
            row_partner,
            beside,
        )
        waiting = [share]
        y_planes.append([to_distance(turned, distance) for distance in range(col_count)])
    last = gather(tie(waiting, [x_cols[-1][0]]))
    y_cols.append((last, 0))
    group_rows = part * per_group

    def scale_of(total):
        total = lax.optimization_barrier(total) / sample_total + 1e-06
        return lax.optimization_barrier(total.astype(jnp.bfloat16)).astype(jnp.float32)

    row_sum, col_sum = sums
    col_sum = col_sum + square_sum([block[:, :group_rows] for block, _ in x_cols[1:]], 1)
    row_rate = (step_size[0] * lax.rsqrt(scale_of(row_sum)))[:, None]
    col_rate = lax.rsqrt(scale_of(col_sum)).reshape(1, lane_tiles * LANES)

    planes = (col_index - jnp.arange(col_count, dtype=jnp.int32) + col_count) % col_count
    info = jnp.concatenate([row_index[None], planes])
    x_entries = [(block, at * per_group + s) for block, at in x_cols for s in range(per_group)]
    updated = omega3
    for k in range(GROUPS):
        block, at = y_cols[k]
        first = k * per_group
        updated = update(
            k,
            x_turned[first : first + per_group],
            y_planes[k],
            [(block, at * per_group + s) for s in range(per_group)],
            x_entries,
            updated,
            row_rate,
            col_rate,
            signs[0] if k == GROUPS - 1 else None,
            info,
            0.5 / sample_total,
        )
    return updated.reshape(omega.shape)


def solution(mesh):
    in_specs = (P("col", "row"), P("row", None, "col", None), P("row", None, "col", None), P())
    out_specs = P("row", None, "col", None)
    return jax.shard_map(body, mesh=mesh, in_specs=in_specs, out_specs=out_specs, check_vma=False)
```

```python
import functools

import jax
import jax.numpy as jnp
from jax import lax
from jax.experimental import pallas as pl
from jax.experimental.pallas import tpu as pltpu
from jax.sharding import PartitionSpec as P

PENALTY = 0.05
LANES = 128
SUBS = 8
GROUPS = 2
PIECES = 2
X_STEPS = (1, 2, 1)
MIB = 1 << 20


def convert_kernel(omega_ref, out_ref):
    rows = omega_ref.shape[0]
    blocks, _, width = out_ref.shape
    flat = omega_ref.reshape(rows * SUBS, LANES)
    per_block = width // LANES
    for c in range(SUBS):
        piece = flat[pl.ds(c, rows, stride=SUBS), :].astype(jnp.bfloat16)
        lane = (c % per_block) * LANES
        out_ref[c // per_block, :, lane : lane + LANES] = piece


def convert(omega3, group_count, sub_width):
    row_total, lane_tiles, _ = omega3.shape
    tile = min(512, row_total)
    blocks = SUBS * LANES // sub_width
    return pl.pallas_call(
        convert_kernel,
        grid=(row_total // tile, lane_tiles // SUBS),
        in_specs=[pl.BlockSpec((tile, SUBS, LANES), lambda i, j: (i, j, 0))],
        out_specs=pl.BlockSpec((blocks, tile, sub_width), lambda i, j: (j, i, 0)),
        out_shape=jax.ShapeDtypeStruct((group_count, row_total, sub_width), jnp.bfloat16),
        compiler_params=pltpu.CompilerParams(vmem_limit_bytes=32 * MIB),
        cost_estimate=pl.CostEstimate(flops=0, bytes_accessed=omega3.size * 6, transcendentals=0),
        name="omega_to_bf16",
    )(omega3)


def turn_kernel(*refs):
    refs[-1][...] = jnp.concatenate([r[...] for r in refs[:-1]], axis=0).T


def turn(pieces, width):
    rows, total = pieces[0].shape
    count = rows * len(pieces)
    return pl.pallas_call(
        turn_kernel,
        grid=(total // width,),
        in_specs=[pl.BlockSpec((rows, width), lambda i: (0, i)) for _ in pieces],
        out_specs=pl.BlockSpec((width, count), lambda i: (i, 0)),
        out_shape=jax.ShapeDtypeStruct((total, count), pieces[0].dtype),
        compiler_params=pltpu.CompilerParams(vmem_limit_bytes=16 * MIB),
        cost_estimate=pl.CostEstimate(
            flops=0, bytes_accessed=4 * count * total, transcendentals=0
        ),
        name="turn",
    )(*pieces)


def tie(values, done):
    return lax.optimization_barrier((values, done))[0] if done else values


def multiply_rows(x_refs, weight):
    rows = jnp.concatenate([x[...] for x in x_refs], axis=0)
    return jnp.dot(rows, weight, preferred_element_type=jnp.float32)


def sent_kernel(count, order_ref, *refs):
    x_refs, w_ref, out_ref = refs[:count], refs[count], refs[count + 1]
    out_ref[0] = multiply_rows(x_refs, w_ref[0]).astype(jnp.bfloat16)


def reversed_bits(value, bits):
    return sum(((value >> b) & 1) << (bits - 1 - b) for b in range(bits))


def kept_kernel(count, bits, order_ref, *refs):
    x_refs, w_ref, other_ref = refs[:count], refs[count], refs[count + 1]
    halves = (refs[count + 2 : count + 4], refs[count + 4 : count + 6])
    total = multiply_rows(x_refs, w_ref[0]) + other_ref[0].astype(jnp.float32)
    rows = total.shape[0] // 2
    step = pl.program_id(0)
    split = 1 << (bits - 1)
    for relative in range(1 << bits):

        @pl.when(step == relative)
        def _():
            for h, (sent_ref, kept_ref) in enumerate(halves):
                place = relative if h else reversed_bits(relative, bits)
                target = sent_ref if place >= split else kept_ref
                target[place % split] = total[h * rows : (h + 1) * rows].astype(target.dtype)


def pair_products(xs, weights, order_sent, order_kept, row_partner, beside):
    count = len(xs)
    rows, depth = xs[0].shape
    group_count, _, width = weights.shape
    blocks = group_count // 2
    bits = blocks.bit_length() - 1
    total_rows = count * rows
    x_spec = pl.BlockSpec((rows, depth), lambda g, order: (0, 0))
    w_spec = pl.BlockSpec((1, depth, width), lambda g, order: (order[g], 0, 0))
    block_spec = pl.BlockSpec((1, total_rows, width), lambda g, order: (g, 0, 0))
    cost = pl.CostEstimate(
        flops=2 * total_rows * depth * blocks * width,
        bytes_accessed=weights.size + 2 * count * xs[0].size + 2 * blocks * total_rows * width,
        transcendentals=0,
    )
    params = pltpu.CompilerParams(vmem_limit_bytes=48 * MIB)
    sent = pl.pallas_call(
        functools.partial(sent_kernel, count),
        grid_spec=pltpu.PrefetchScalarGridSpec(
            num_scalar_prefetch=1,
            grid=(blocks,),
            in_specs=[x_spec] * count + [w_spec],
            out_specs=block_spec,
        ),
        out_shape=jax.ShapeDtypeStruct((blocks, total_rows, width), jnp.bfloat16),
        compiler_params=params,
        cost_estimate=cost,
        name="products_sent",
    )(order_sent, *xs, weights)
    other = tie(lax.ppermute(sent, "row", row_partner(1)), beside(0, sent))
    half = (blocks // 2, total_rows // 2, width)
    half_spec = pl.BlockSpec(half, lambda g, order: (0, 0, 0))
    outs = pl.pallas_call(
        functools.partial(kept_kernel, count, bits),
        grid_spec=pltpu.PrefetchScalarGridSpec(
            num_scalar_prefetch=1,
            grid=(blocks,),
            in_specs=[x_spec] * count + [w_spec, block_spec],
            out_specs=[half_spec] * 4,
        ),
        out_shape=[
            jax.ShapeDtypeStruct(half, jnp.bfloat16),
            jax.ShapeDtypeStruct(half, jnp.float32),
        ]
        * 2,
        compiler_params=params,
        cost_estimate=cost,
        name="products_kept",
    )(order_kept, *xs, weights, other)
    return [(outs[0], outs[1]), (outs[2], outs[3])]


def halve_kernel(split, *refs):
    for h in range(2):
        kept_ref, other_ref, next_sent, next_kept = refs[2 * h], refs[2 * h + 1], refs[4 + 2 * h], refs[5 + 2 * h]
        next_kept[...] = kept_ref[:split] + other_ref[:split].astype(jnp.float32)
        total = kept_ref[split:] + other_ref[split:].astype(jnp.float32)
        next_sent[...] = total.astype(jnp.bfloat16)


def halve(pieces, others):
    kept = pieces[0][1]
    split = kept.shape[0] // 2
    shape = (split,) + kept.shape[1:]
    outs = pl.pallas_call(
        functools.partial(halve_kernel, split),
        out_shape=[
            jax.ShapeDtypeStruct(shape, jnp.bfloat16),
            jax.ShapeDtypeStruct(shape, jnp.float32),
        ]
        * 2,
        compiler_params=pltpu.CompilerParams(vmem_limit_bytes=32 * MIB),
        cost_estimate=pl.CostEstimate(flops=0, bytes_accessed=18 * kept.size, transcendentals=0),
        name="halve",
    )(pieces[0][1], others[0], pieces[1][1], others[1])
    return [(outs[0], outs[1]), (outs[2], outs[3])]


def share_kernel(*refs):
    share_ref, turned_ref = refs[4:]
    rows = refs[0].shape[1]
    for h in range(2):
        total = refs[2 * h][0] + refs[2 * h + 1][0].astype(jnp.float32)
        share_ref[h * rows : (h + 1) * rows, :] = total.astype(jnp.bfloat16)
    turned_ref[...] = share_ref[...].T


def finish_share(pieces, others):
    _, rows, width = pieces[0][1].shape
    return pl.pallas_call(
        share_kernel,
        out_shape=[
            jax.ShapeDtypeStruct((2 * rows, width), jnp.bfloat16),
            jax.ShapeDtypeStruct((width, 2 * rows), jnp.bfloat16),
        ],
        compiler_params=pltpu.CompilerParams(vmem_limit_bytes=24 * MIB),
        cost_estimate=pl.CostEstimate(
            flops=0, bytes_accessed=20 * rows * width, transcendentals=0
        ),
        name="share",
    )(pieces[0][1], others[0], pieces[1][1], others[1])


def sum_over_rows(xs, weights, order_sent, order_kept, row_partner, beside):
    pieces = pair_products(xs, weights, order_sent, order_kept, row_partner, beside)
    bits = weights.shape[0].bit_length() - 2
    for level in range(bits):
        masks = (2 << level, 1 << (bits - level))
        others = [
            lax.ppermute(sent, "row", row_partner(mask)) for (sent, _), mask in zip(pieces, masks)
        ]
        others = tie(others, beside(level + 1, pieces[0][0]))
        if level < bits - 1:
            pieces = halve(pieces, others)
    share, turned = finish_share(pieces, others)
    return share, turned


def narrow_kernel(sign_ref, out_ref):
    rows = sign_ref.shape[0]
    flat = sign_ref.reshape(rows * SUBS, LANES)
    for c in range(SUBS):
        piece = flat[pl.ds(c, rows, stride=SUBS), :]
        out_ref[:, c * LANES : (c + 1) * LANES] = piece.astype(jnp.int8)


def narrow(sign3):
    row_total, lane_tiles, _ = sign3.shape
    tile = min(512, row_total)
    return pl.pallas_call(
        narrow_kernel,
        grid=(row_total // tile, lane_tiles // SUBS),
        in_specs=[pl.BlockSpec((tile, SUBS, LANES), lambda i, j: (i, j, 0))],
        out_specs=pl.BlockSpec((tile, SUBS * LANES), lambda i, j: (i, j)),
        out_shape=jax.ShapeDtypeStruct((row_total, lane_tiles * LANES), jnp.int8),
        compiler_params=pltpu.CompilerParams(vmem_limit_bytes=32 * MIB),
        cost_estimate=pl.CostEstimate(flops=0, bytes_accessed=sign3.size * 5, transcendentals=0),
        name="narrow_signs",
    )(sign3)


def update_kernel(sizes, group, sub_width, scale, last, info_ref, *refs):
    col_count, per_group = sizes
    xs, refs = refs[:per_group], refs[per_group:]
    ys, refs = refs[:col_count], refs[col_count:]
    y_cols, refs = refs[:per_group], refs[per_group:]
    x_cols, refs = refs[:col_count], refs[col_count:]
    old_ref, row_ref, col_ref = refs[:3]
    if last:
        sign_ref, out_ref, cross_ref = refs[3:]
    else:
        out_ref = refs[3]
    rows = row_ref.shape[0]
    per_block = sub_width // LANES
    blocks = SUBS // per_block
    width = min(sub_width, 512)
    distance = pl.program_id(1)
    native = (out_ref if last else old_ref).reshape(rows * SUBS, LANES)
    row_rate = jnp.broadcast_to(row_ref[...], (rows, LANES))
    row_smooth = row_rate * scale
    row_shift = row_rate * PENALTY

    for value in range(col_count):

        @pl.when(distance == value)
        def _():
            met = [x_cols[(group * per_group + s + value) % col_count] for s in range(per_group)]
            left = jnp.concatenate([x[...] for x in xs] + [ys[value][...]], axis=1)
            for first in range(0, SUBS * LANES, width):
                b, at = first // sub_width, first % sub_width
                right = jnp.concatenate(
                    [r[b, :, at : at + width] for r in (*y_cols, *met)], axis=0
                )
                total = jnp.dot(left, right, preferred_element_type=jnp.float32)
                if last and value == 0:
                    cross_ref[:, first : first + width] = total
                for lane in range(0, width, LANES):
                    columns = slice(first + lane, first + lane + LANES)
                    spot = pl.ds((first + lane) // LANES, rows, stride=SUBS)
                    col_rate = col_ref[:, columns]
                    taken = (row_smooth * col_rate) * total[:, lane : lane + LANES]
                    if last:
                        trial = old_ref[:, columns].astype(jnp.float32) - taken
                        sign = sign_ref[:, columns].astype(jnp.float32)
                        shift = row_shift * col_rate
                        native[spot, :] = sign * jnp.maximum(sign * trial - shift, 0.0)
                    else:
                        out_ref[:, columns] = (native[spot, :] - taken).astype(out_ref.dtype)

    if last:
        for b in range(blocks):

            @pl.when(jnp.logical_and(distance == 0, pl.program_id(0) * blocks + b == info_ref[0]))
            def _():
                for lane in range(0, sub_width, LANES):
                    first = b * sub_width + lane
                    columns = slice(first, first + LANES)
                    spot = pl.ds(first // LANES, rows, stride=SUBS)
                    rate = row_rate * col_ref[:, columns]
                    trial = old_ref[:, columns].astype(jnp.float32)
                    trial = trial - rate * (cross_ref[:, columns] * scale)
                    value = 0.5 * (trial + jnp.sqrt(trial * trial + 4.0 * rate))
                    row_ids = lax.broadcasted_iota(jnp.int32, (rows, LANES), 0)
                    col_ids = lax.broadcasted_iota(jnp.int32, (rows, LANES), 1) + lane
                    native[spot, :] = jnp.where(row_ids == col_ids, value, native[spot, :])


def update(group, xs, ys, y_cols, x_cols, old, row_rate, col_rate, signs, info, scale):
    row_total = row_rate.shape[0]
    lane_tiles = col_rate.shape[1] // LANES
    part = xs[0].shape[1]
    tile = sub_width = ys[0].shape[0]
    blocks = SUBS * LANES // sub_width
    last = signs is not None
    sizes = (len(ys), len(xs))
    native_block = pl.BlockSpec((tile, SUBS, LANES), lambda j, d, p: (p[1 + d], j, 0))
    row_block = pl.BlockSpec((tile, SUBS * LANES), lambda j, d, p: (p[1 + d], j))
    columns = list(y_cols) + list(x_cols)
    operands = [*xs, *ys, *[b for b, _ in columns], old, row_rate, col_rate]
    if last:
        result = jax.ShapeDtypeStruct((row_total, lane_tiles, LANES), jnp.float32)
    else:
        result = jax.ShapeDtypeStruct((row_total, lane_tiles * LANES), jnp.bfloat16)
    elements = row_total * lane_tiles * LANES
    return pl.pallas_call(
        functools.partial(update_kernel, sizes, group, sub_width, scale, last),
        grid_spec=pltpu.PrefetchScalarGridSpec(
            num_scalar_prefetch=1,
            grid=(lane_tiles // SUBS, row_total // tile),
            in_specs=[pl.BlockSpec((tile, part), lambda j, d, p: (p[1 + d], 0)) for _ in xs]
            + [pl.BlockSpec(y.shape, lambda j, d, p: (0, 0)) for y in ys]
            + [
                pl.BlockSpec((blocks, part, sub_width), lambda j, d, p, at=at: (j, at, 0))
                for _, at in columns
            ]
            + [
                row_block if last else native_block,
                pl.BlockSpec((tile, 1), lambda j, d, p: (p[1 + d], 0)),
                pl.BlockSpec((1, SUBS * LANES), lambda j, d, p: (0, j)),
            ]
            + [row_block] * last,
            out_specs=native_block if last else row_block,
            scratch_shapes=[pltpu.VMEM((tile, SUBS * LANES), jnp.float32)] * last,
        ),
        out_shape=result,
        compiler_params=pltpu.CompilerParams(vmem_limit_bytes=56 * MIB),
        cost_estimate=pl.CostEstimate(
            flops=4 * part * len(xs) * elements, bytes_accessed=elements * 8, transcendentals=0
        ),
        name="last_terms" if last else "first_terms",
    )(info, *operands, *([signs] if last else []))


def body(samples, omega, sign_mask, step_size):
    row_total, group_count, _, sub_width = omega.shape
    lane_tiles = group_count * sub_width // LANES
    row_count = lax.axis_size("row")
    col_count = lax.axis_size("col")
    row_index = lax.axis_index("row").astype(jnp.int32)
    col_index = lax.axis_index("col").astype(jnp.int32)
    part = samples.shape[0]
    sample_total = part * col_count
    per_group = col_count // GROUPS
    omega3 = omega.reshape(row_total, lane_tiles, LANES)
    sign3 = sign_mask.reshape(row_total, lane_tiles, LANES)

    def row_partner(mask):
        return [(r, r ^ mask) for r in range(row_count)]

    ring = [(c, (c + 1) % col_count) for c in range(col_count)]
    relative = jnp.arange(row_count // 2, dtype=jnp.int32)
    order_kept = ((row_index >> 1) ^ relative) * 2 + (row_index & 1)
    order_sent = order_kept ^ 1

    xs = [[samples[k * part // PIECES : (k + 1) * part // PIECES] for k in range(PIECES)]]
    x_turned, y_planes = [], []
    weights = convert(omega3, group_count, sub_width)

    def advance():
        if len(xs[-1]) == PIECES:
            xs.append([])
        done = lax.ppermute(xs[-2][len(xs[-1])], "col", ring)
        xs[-1].append(done)
        return done

    def to_distance(y, distance):
        if not distance:
            return y
        return lax.ppermute(y, "col", [(c, (c + distance) % col_count) for c in range(col_count)])

    def square_sum(pieces, axis):
        return sum(jnp.sum(jnp.square(p.astype(jnp.float32)), axis=axis) for p in pieces)

    def entry_rows(block, at):
        return block[:, at * part : (at + 1) * part]

    sums, signs = [], []

    def complete(length):
        return len(xs) >= length and len(xs[length - 1]) == PIECES

    def columns(entries):
        return [
            lax.dynamic_slice_in_dim(x, col_index * sub_width, sub_width, 1)
            for pieces in entries
            for x in pieces
        ]

    def gather(rows):
        return lax.all_gather(jnp.concatenate(rows, axis=0), "row", axis=0, tiled=False)

    x_cols, y_cols, waiting, marks = [], [], [], []
    for k in range(GROUPS):
        first = k * per_group
        while not complete(first + per_group):
            advance()
        if not k:
            xs[-1] = tie(xs[-1], [weights])
        group = xs[first : first + per_group]
        if k:
            block = gather(columns(tie(group[:-1], [marks[1], x_cols[-1][0]])))
            x_cols.extend((block, s) for s in range(per_group - 1))
            block = gather(tie(columns(group[-1:]) + waiting, [block]))
            x_cols.append((block, 0))
            y_cols.append([(block, 1 + s) for s in range(per_group)])
        else:
            block = gather(columns(group))
            x_cols.extend((block, s) for s in range(per_group))

        def beside(exchange, sent):
            done = []
            marks.append(sent)
            if exchange == 0:
                x_turned.extend(turn(x, sub_width) for x in group)
                done.extend(x_turned[first:])
            for _ in range(X_STEPS[min(exchange, len(X_STEPS) - 1)]):
                if not complete(col_count):
                    done.append(advance())
            if y_planes and exchange == 1:
                done.append(y_planes[0][1])
                signs.append(narrow(tie(sign3, [sent])))
                done.extend(signs)
            if y_planes and exchange == 2:
                done.extend(y_planes[0][2:])
                sums.append(square_sum([x for pieces in xs for x in pieces], 0))
                sums.append(square_sum([entry_rows(*entry) for entry in x_cols[:-1]], 1))
                done.extend(sums)
            return done

        share, turned = sum_over_rows(
            [x for pieces in group for x in pieces],
            weights,
            order_sent,
            order_kept,
            row_partner,
            beside,
        )
        waiting = [share]
        y_planes.append([to_distance(turned, distance) for distance in range(col_count)])
    last = gather(tie(waiting, [x_cols[-1][0]]))
    y_cols.append([(last, s) for s in range(per_group)])

    def scale_of(total):
        total = lax.optimization_barrier(total) / sample_total + 1e-06
        return lax.optimization_barrier(total.astype(jnp.bfloat16)).astype(jnp.float32)

    row_sum, col_sum = sums
    col_sum = col_sum + square_sum([entry_rows(*x_cols[-1])], 1)
    row_rate = (step_size[0] * lax.rsqrt(scale_of(row_sum)))[:, None]
    col_rate = lax.rsqrt(scale_of(col_sum)).reshape(1, lane_tiles * LANES)

    planes = (col_index - jnp.arange(col_count, dtype=jnp.int32) + col_count) % col_count
    info = jnp.concatenate([row_index[None], planes])
    updated = omega3
    for k in range(GROUPS):
        first = k * per_group
        updated = update(
            k,
            x_turned[first : first + per_group],
            y_planes[k],
            y_cols[k],
            x_cols,
            updated,
            row_rate,
            col_rate,
            signs[0] if k == GROUPS - 1 else None,
            info,
            0.5 / sample_total,
        )
    return updated.reshape(omega.shape)


def solution(mesh):
    in_specs = (P("col", "row"), P("row", None, "col", None), P("row", None, "col", None), P())
    out_specs = P("row", None, "col", None)
    return jax.shard_map(body, mesh=mesh, in_specs=in_specs, out_specs=out_specs, check_vma=False)
```

```python
import functools

import jax
import jax.numpy as jnp
from jax import lax
from jax.experimental import pallas as pl
from jax.experimental.pallas import tpu as pltpu
from jax.sharding import PartitionSpec as P

PENALTY = 0.05
LANES = 128
SUBS = 8
GROUPS = 2
PIECES = 2
X_STEPS = (1, 2, 1)
MIB = 1 << 20


def convert_kernel(omega_ref, out_ref):
    rows = omega_ref.shape[0]
    blocks, _, width = out_ref.shape
    flat = omega_ref.reshape(rows * SUBS, LANES)
    per_block = width // LANES
    for c in range(SUBS):
        piece = flat[pl.ds(c, rows, stride=SUBS), :].astype(jnp.bfloat16)
        lane = (c % per_block) * LANES
        out_ref[c // per_block, :, lane : lane + LANES] = piece


def convert(omega3, group_count, sub_width):
    row_total, lane_tiles, _ = omega3.shape
    tile = min(512, row_total)
    blocks = SUBS * LANES // sub_width
    return pl.pallas_call(
        convert_kernel,
        grid=(row_total // tile, lane_tiles // SUBS),
        in_specs=[pl.BlockSpec((tile, SUBS, LANES), lambda i, j: (i, j, 0))],
        out_specs=pl.BlockSpec((blocks, tile, sub_width), lambda i, j: (j, i, 0)),
        out_shape=jax.ShapeDtypeStruct((group_count, row_total, sub_width), jnp.bfloat16),
        compiler_params=pltpu.CompilerParams(vmem_limit_bytes=32 * MIB),
        cost_estimate=pl.CostEstimate(flops=0, bytes_accessed=omega3.size * 6, transcendentals=0),
        name="omega_to_bf16",
    )(omega3)


def turn_kernel(*refs):
    refs[-1][...] = jnp.concatenate([r[...] for r in refs[:-1]], axis=0).T


def turn(pieces, width):
    rows, total = pieces[0].shape
    count = rows * len(pieces)
    return pl.pallas_call(
        turn_kernel,
        grid=(total // width,),
        in_specs=[pl.BlockSpec((rows, width), lambda i: (0, i)) for _ in pieces],
        out_specs=pl.BlockSpec((width, count), lambda i: (i, 0)),
        out_shape=jax.ShapeDtypeStruct((total, count), pieces[0].dtype),
        compiler_params=pltpu.CompilerParams(vmem_limit_bytes=16 * MIB),
        cost_estimate=pl.CostEstimate(
            flops=0, bytes_accessed=4 * count * total, transcendentals=0
        ),
        name="turn",
    )(*pieces)


def tie(values, done):
    return lax.optimization_barrier((values, done))[0] if done else values


def multiply_rows(x_refs, weight):
    rows = jnp.concatenate([x[...] for x in x_refs], axis=0)
    return jnp.dot(rows, weight, preferred_element_type=jnp.float32)


def sent_kernel(count, order_ref, *refs):
    x_refs, w_ref, out_ref = refs[:count], refs[count], refs[count + 1]
    out_ref[0] = multiply_rows(x_refs, w_ref[0]).astype(jnp.bfloat16)


def reversed_bits(value, bits):
    return sum(((value >> b) & 1) << (bits - 1 - b) for b in range(bits))


def kept_kernel(count, other_count, bits, order_ref, *refs):
    x_refs, w_ref, refs = refs[:count], refs[count], refs[count + 1 :]
    other_refs, refs = refs[:other_count], refs[other_count:]
    halves = (refs[:2], refs[2:])
    other = jnp.concatenate([r[0] for r in other_refs], axis=0)
    total = multiply_rows(x_refs, w_ref[0]) + other.astype(jnp.float32)
    rows = total.shape[0] // 2
    step = pl.program_id(0)
    split = 1 << (bits - 1)
    for relative in range(1 << bits):

        @pl.when(step == relative)
        def _():
            for h, (sent_ref, kept_ref) in enumerate(halves):
                place = relative if h else reversed_bits(relative, bits)
                target = sent_ref if place >= split else kept_ref
                target[place % split] = total[h * rows : (h + 1) * rows].astype(target.dtype)


def product_parts(xs, weights):
    rows, depth = xs[0].shape
    group_count, _, width = weights.shape
    blocks = group_count // 2
    total_rows = len(xs) * rows
    x_spec = pl.BlockSpec((rows, depth), lambda g, order: (0, 0))
    w_spec = pl.BlockSpec((1, depth, width), lambda g, order: (order[g], 0, 0))
    cost = pl.CostEstimate(
        flops=2 * total_rows * depth * blocks * width,
        bytes_accessed=weights.size + 2 * len(xs) * xs[0].size + 2 * blocks * total_rows * width,
        transcendentals=0,
    )
    params = pltpu.CompilerParams(vmem_limit_bytes=48 * MIB)
    return blocks, total_rows, width, [x_spec] * len(xs) + [w_spec], cost, params


def products_sent(xs, weights, order_sent):
    blocks, total_rows, width, specs, cost, params = product_parts(xs, weights)
    return pl.pallas_call(
        functools.partial(sent_kernel, len(xs)),
        grid_spec=pltpu.PrefetchScalarGridSpec(
            num_scalar_prefetch=1,
            grid=(blocks,),
            in_specs=specs,
            out_specs=pl.BlockSpec((1, total_rows, width), lambda g, order: (g, 0, 0)),
        ),
        out_shape=jax.ShapeDtypeStruct((blocks, total_rows, width), jnp.bfloat16),
        compiler_params=params,
        cost_estimate=cost,
        name="products_sent",
    )(order_sent, *xs, weights)


def pair_products(xs, weights, sents, order_kept, row_partner, beside):
    blocks, total_rows, width, specs, cost, params = product_parts(xs, weights)
    bits = blocks.bit_length() - 1
    others = tie([lax.ppermute(s, "row", row_partner(1)) for s in sents], beside(0, sents[-1]))
    half = (blocks // 2, total_rows // 2, width)
    half_spec = pl.BlockSpec(half, lambda g, order: (0, 0, 0))
    outs = pl.pallas_call(
        functools.partial(kept_kernel, len(xs), len(others), bits),
        grid_spec=pltpu.PrefetchScalarGridSpec(
            num_scalar_prefetch=1,
            grid=(blocks,),
            in_specs=specs
            + [
                pl.BlockSpec((1, other.shape[1], width), lambda g, order: (g, 0, 0))
                for other in others
            ],
            out_specs=[half_spec] * 4,
        ),
        out_shape=[
            jax.ShapeDtypeStruct(half, jnp.bfloat16),
            jax.ShapeDtypeStruct(half, jnp.float32),
        ]
        * 2,
        compiler_params=params,
        cost_estimate=cost,
        name="products_kept",
    )(order_kept, *xs, weights, *others)
    return [(outs[0], outs[1]), (outs[2], outs[3])]


def halve_kernel(split, *refs):
    for h in range(2):
        kept_ref, other_ref, next_sent, next_kept = refs[2 * h], refs[2 * h + 1], refs[4 + 2 * h], refs[5 + 2 * h]
        next_kept[...] = kept_ref[:split] + other_ref[:split].astype(jnp.float32)
        total = kept_ref[split:] + other_ref[split:].astype(jnp.float32)
        next_sent[...] = total.astype(jnp.bfloat16)


def halve(pieces, others):
    kept = pieces[0][1]
    split = kept.shape[0] // 2
    shape = (split,) + kept.shape[1:]
    outs = pl.pallas_call(
        functools.partial(halve_kernel, split),
        out_shape=[
            jax.ShapeDtypeStruct(shape, jnp.bfloat16),
            jax.ShapeDtypeStruct(shape, jnp.float32),
        ]
        * 2,
        compiler_params=pltpu.CompilerParams(vmem_limit_bytes=32 * MIB),
        cost_estimate=pl.CostEstimate(flops=0, bytes_accessed=18 * kept.size, transcendentals=0),
        name="halve",
    )(pieces[0][1], others[0], pieces[1][1], others[1])
    return [(outs[0], outs[1]), (outs[2], outs[3])]


def share_kernel(*refs):
    share_ref, turned_ref = refs[4:]
    rows = refs[0].shape[1]
    for h in range(2):
        total = refs[2 * h][0] + refs[2 * h + 1][0].astype(jnp.float32)
        share_ref[h * rows : (h + 1) * rows, :] = total.astype(jnp.bfloat16)
    turned_ref[...] = share_ref[...].T


def finish_share(pieces, others):
    _, rows, width = pieces[0][1].shape
    return pl.pallas_call(
        share_kernel,
        out_shape=[
            jax.ShapeDtypeStruct((2 * rows, width), jnp.bfloat16),
            jax.ShapeDtypeStruct((width, 2 * rows), jnp.bfloat16),
        ],
        compiler_params=pltpu.CompilerParams(vmem_limit_bytes=24 * MIB),
        cost_estimate=pl.CostEstimate(
            flops=0, bytes_accessed=20 * rows * width, transcendentals=0
        ),
        name="share",
    )(pieces[0][1], others[0], pieces[1][1], others[1])


def sum_over_rows(xs, weights, sents, order_kept, row_partner, beside):
    pieces = pair_products(xs, weights, sents, order_kept, row_partner, beside)
    bits = weights.shape[0].bit_length() - 2
    for level in range(bits):
        masks = (2 << level, 1 << (bits - level))
        others = [
            lax.ppermute(sent, "row", row_partner(mask)) for (sent, _), mask in zip(pieces, masks)
        ]
        others = tie(others, beside(level + 1, pieces[0][0]))
        if level < bits - 1:
            pieces = halve(pieces, others)
    share, turned = finish_share(pieces, others)
    return share, turned


def narrow_kernel(sign_ref, out_ref):
    rows = sign_ref.shape[0]
    flat = sign_ref.reshape(rows * SUBS, LANES)
    for c in range(SUBS):
        piece = flat[pl.ds(c, rows, stride=SUBS), :]
        out_ref[:, c * LANES : (c + 1) * LANES] = piece.astype(jnp.int8)


def narrow(sign3):
    row_total, lane_tiles, _ = sign3.shape
    tile = min(512, row_total)
    return pl.pallas_call(
        narrow_kernel,
        grid=(row_total // tile, lane_tiles // SUBS),
        in_specs=[pl.BlockSpec((tile, SUBS, LANES), lambda i, j: (i, j, 0))],
        out_specs=pl.BlockSpec((tile, SUBS * LANES), lambda i, j: (i, j)),
        out_shape=jax.ShapeDtypeStruct((row_total, lane_tiles * LANES), jnp.int8),
        compiler_params=pltpu.CompilerParams(vmem_limit_bytes=32 * MIB),
        cost_estimate=pl.CostEstimate(flops=0, bytes_accessed=sign3.size * 5, transcendentals=0),
        name="narrow_signs",
    )(sign3)


def update_kernel(sizes, group, sub_width, scale, last, info_ref, *refs):
    col_count, per_group = sizes
    xs, refs = refs[:per_group], refs[per_group:]
    ys, refs = refs[:col_count], refs[col_count:]
    y_cols, refs = refs[:per_group], refs[per_group:]
    x_cols, refs = refs[:col_count], refs[col_count:]
    old_ref, row_ref, col_ref = refs[:3]
    if last:
        sign_ref, out_ref, cross_ref = refs[3:]
    else:
        out_ref = refs[3]
    rows = row_ref.shape[0]
    per_block = sub_width // LANES
    blocks = SUBS // per_block
    width = min(sub_width, 256)
    distance = pl.program_id(1)
    native = (out_ref if last else old_ref).reshape(rows * SUBS, LANES)
    row_rate = jnp.broadcast_to(row_ref[...], (rows, LANES))
    row_smooth = row_rate * scale
    row_shift = row_rate * PENALTY

    for value in range(col_count):

        @pl.when(distance == value)
        def _():
            met = [x_cols[(group * per_group + s + value) % col_count] for s in range(per_group)]
            left = jnp.concatenate([x[...] for x in xs] + [ys[value][...]], axis=1)
            for first in range(0, SUBS * LANES, width):
                b, at = first // sub_width, first % sub_width
                right = jnp.concatenate(
                    [r[b, :, at : at + width] for r in (*y_cols, *met)], axis=0
                )
                total = jnp.dot(left, right, preferred_element_type=jnp.float32)
                if last and value == 0:
                    cross_ref[:, first : first + width] = total
                for lane in range(0, width, LANES):
                    columns = slice(first + lane, first + lane + LANES)
                    spot = pl.ds((first + lane) // LANES, rows, stride=SUBS)
                    col_rate = col_ref[:, columns]
                    taken = (row_smooth * col_rate) * total[:, lane : lane + LANES]
                    if last:
                        trial = old_ref[:, columns].astype(jnp.float32) - taken
                        sign = sign_ref[:, columns].astype(jnp.float32)
                        shift = row_shift * col_rate
                        native[spot, :] = sign * jnp.maximum(sign * trial - shift, 0.0)
                    else:
                        out_ref[:, columns] = (native[spot, :] - taken).astype(out_ref.dtype)

    if last:
        for b in range(blocks):

            @pl.when(jnp.logical_and(distance == 0, pl.program_id(0) * blocks + b == info_ref[0]))
            def _():
                for lane in range(0, sub_width, LANES):
                    first = b * sub_width + lane
                    columns = slice(first, first + LANES)
                    spot = pl.ds(first // LANES, rows, stride=SUBS)
                    rate = row_rate * col_ref[:, columns]
                    trial = old_ref[:, columns].astype(jnp.float32)
                    trial = trial - rate * (cross_ref[:, columns] * scale)
                    value = 0.5 * (trial + jnp.sqrt(trial * trial + 4.0 * rate))
                    row_ids = lax.broadcasted_iota(jnp.int32, (rows, LANES), 0)
                    col_ids = lax.broadcasted_iota(jnp.int32, (rows, LANES), 1) + lane
                    native[spot, :] = jnp.where(row_ids == col_ids, value, native[spot, :])


def update(group, xs, ys, y_cols, x_cols, old, row_rate, col_rate, signs, info, scale):
    row_total = row_rate.shape[0]
    lane_tiles = col_rate.shape[1] // LANES
    part = xs[0].shape[1]
    tile = sub_width = ys[0].shape[0]
    blocks = SUBS * LANES // sub_width
    last = signs is not None
    sizes = (len(ys), len(xs))
    native_block = pl.BlockSpec((tile, SUBS, LANES), lambda j, d, p: (p[1 + d], j, 0))
    row_block = pl.BlockSpec((tile, SUBS * LANES), lambda j, d, p: (p[1 + d], j))
    columns = list(y_cols) + list(x_cols)
    operands = [*xs, *ys, *[b for b, _ in columns], old, row_rate, col_rate]
    if last:
        result = jax.ShapeDtypeStruct((row_total, lane_tiles, LANES), jnp.float32)
    else:
        result = jax.ShapeDtypeStruct((row_total, lane_tiles * LANES), jnp.bfloat16)
    elements = row_total * lane_tiles * LANES
    return pl.pallas_call(
        functools.partial(update_kernel, sizes, group, sub_width, scale, last),
        grid_spec=pltpu.PrefetchScalarGridSpec(
            num_scalar_prefetch=1,
            grid=(lane_tiles // SUBS, row_total // tile),
            in_specs=[pl.BlockSpec((tile, part), lambda j, d, p: (p[1 + d], 0)) for _ in xs]
            + [pl.BlockSpec(y.shape, lambda j, d, p: (0, 0)) for y in ys]
            + [
                pl.BlockSpec((blocks, part, sub_width), lambda j, d, p, at=at: (j, at, 0))
                for _, at in columns
            ]
            + [
                row_block if last else native_block,
                pl.BlockSpec((tile, 1), lambda j, d, p: (p[1 + d], 0)),
                pl.BlockSpec((1, SUBS * LANES), lambda j, d, p: (0, j)),
            ]
            + [row_block] * last,
            out_specs=native_block if last else row_block,
            scratch_shapes=[pltpu.VMEM((tile, SUBS * LANES), jnp.float32)] * last,
        ),
        out_shape=result,
        compiler_params=pltpu.CompilerParams(vmem_limit_bytes=56 * MIB),
        cost_estimate=pl.CostEstimate(
            flops=4 * part * len(xs) * elements, bytes_accessed=elements * 8, transcendentals=0
        ),
        name="last_terms" if last else "first_terms",
    )(info, *operands, *([signs] if last else []))


def body(samples, omega, sign_mask, step_size):
    row_total, group_count, _, sub_width = omega.shape
    lane_tiles = group_count * sub_width // LANES
    row_count = lax.axis_size("row")
    col_count = lax.axis_size("col")
    row_index = lax.axis_index("row").astype(jnp.int32)
    col_index = lax.axis_index("col").astype(jnp.int32)
    part = samples.shape[0]
    sample_total = part * col_count
    per_group = col_count // GROUPS
    omega3 = omega.reshape(row_total, lane_tiles, LANES)
    sign3 = sign_mask.reshape(row_total, lane_tiles, LANES)

    def row_partner(mask):
        return [(r, r ^ mask) for r in range(row_count)]

    ring = [(c, (c + 1) % col_count) for c in range(col_count)]
    relative = jnp.arange(row_count // 2, dtype=jnp.int32)
    order_kept = ((row_index >> 1) ^ relative) * 2 + (row_index & 1)
    order_sent = order_kept ^ 1

    xs = [[samples[k * part // PIECES : (k + 1) * part // PIECES] for k in range(PIECES)]]
    x_turned, y_planes = [], []
    weights = convert(omega3, group_count, sub_width)

    def advance():
        if len(xs[-1]) == PIECES:
            xs.append([])
        done = lax.ppermute(xs[-2][len(xs[-1])], "col", ring)
        xs[-1].append(done)
        return done

    def to_distance(y, distance):
        if not distance:
            return y
        return lax.ppermute(y, "col", [(c, (c + distance) % col_count) for c in range(col_count)])

    def square_sum(pieces, axis):
        return sum(jnp.sum(jnp.square(p.astype(jnp.float32)), axis=axis) for p in pieces)

    sums, signs = [], []

    def complete(length):
        return len(xs) >= length and len(xs[length - 1]) == PIECES

    def gather(rows):
        return lax.all_gather(jnp.concatenate(rows, axis=0), "row", axis=0, tiled=False)

    x_cols, y_cols, waiting = [], [], []
    for k in range(GROUPS):
        first = k * per_group
        while not complete(first + per_group):
            advance()
        sents = []
        if not k:
            sents.append(products_sent(xs[0], weights, order_sent))
            xs[1] = tie(xs[1], sents)
        group = xs[first : first + per_group]
        rest = [x for pieces in group[len(sents) :] for x in pieces]
        sents.append(products_sent(rest, weights, order_sent))
        own = [
            lax.dynamic_slice_in_dim(x, col_index * sub_width, sub_width, 1)
            for pieces in group
            for x in pieces
        ]
        block = gather(own + waiting)
        x_cols.append((block, 0))
        if waiting:
            y_cols.append((block, 1))

        def beside(exchange, sent):
            done = []
            if exchange == 0:
                x_turned.extend(turn(x, sub_width) for x in group)
                done.extend(x_turned[first:])
                done.extend(block for block, _ in x_cols[:-1])
            for _ in range(X_STEPS[min(exchange, len(X_STEPS) - 1)]):
                if not complete(col_count):
                    done.append(advance())
            if y_planes and exchange == 1:
                done.append(y_planes[0][1])
                signs.append(narrow(tie(sign3, [sent])))
                done.extend(signs)
            if y_planes and exchange == 2:
                done.extend(y_planes[0][2:])
                sums.append(square_sum([x for pieces in xs for x in pieces], 0))
                sums.append(square_sum([x_cols[0][0]], 1))
                done.extend(sums)
            return done

        share, turned = sum_over_rows(
            [x for pieces in group for x in pieces],
            weights,
            sents,
            order_kept,
            row_partner,
            beside,
        )
        waiting = [share]
        y_planes.append([to_distance(turned, distance) for distance in range(col_count)])
    last = gather(tie(waiting, [x_cols[-1][0]]))
    y_cols.append((last, 0))
    group_rows = part * per_group

    def scale_of(total):
        total = lax.optimization_barrier(total) / sample_total + 1e-06
        return lax.optimization_barrier(total.astype(jnp.bfloat16)).astype(jnp.float32)

    row_sum, col_sum = sums
    col_sum = col_sum + square_sum([block[:, :group_rows] for block, _ in x_cols[1:]], 1)
    row_rate = (step_size[0] * lax.rsqrt(scale_of(row_sum)))[:, None]
    col_rate = lax.rsqrt(scale_of(col_sum)).reshape(1, lane_tiles * LANES)

    planes = (col_index - jnp.arange(col_count, dtype=jnp.int32) + col_count) % col_count
    info = jnp.concatenate([row_index[None], planes])
    x_entries = [(block, at * per_group + s) for block, at in x_cols for s in range(per_group)]
    updated = omega3
    for k in range(GROUPS):
        block, at = y_cols[k]
        first = k * per_group
        updated = update(
            k,
            x_turned[first : first + per_group],
            y_planes[k],
            [(block, at * per_group + s) for s in range(per_group)],
            x_entries,
            updated,
            row_rate,
            col_rate,
            signs[0] if k == GROUPS - 1 else None,
            info,
            0.5 / sample_total,
        )
    return updated.reshape(omega.shape)


def solution(mesh):
    in_specs = (P("col", "row"), P("row", None, "col", None), P("row", None, "col", None), P())
    out_specs = P("row", None, "col", None)
    return jax.shard_map(body, mesh=mesh, in_specs=in_specs, out_specs=out_specs, check_vma=False)
```
